32 devices in a mesh: fsdp: 16 (over z, y, core), dp: 2 (over x).
Axes of the slice: x: 2, y: 2, z: 4, core: 2. Of those that a mesh axis runs over, the one named last changes fastest.
Arguments:
- patches: bfloat16 [32, 576, 768], P(('fsdp', 'dp')), may hold values from -6 to 6
- masks: int32 [32, 576], P(('fsdp', 'dp')), may hold values from 0 to 1
- groups: int32 [32], P(('fsdp', 'dp')), may hold values from 0 to 1
- w_square: float32 [3, 768, 768], P(None, 'fsdp'), may hold values from -0.5 to 0.5
- w_qkv: float32 [768, 2304], P('fsdp'), may hold values from -0.21875 to 0.21875
- w_up: float32 [768, 3072], P('fsdp'), may hold values from -0.21875 to 0.21875
- w_down: float32 [3072, 768], P(None, 'fsdp'), may hold values from -0.109375 to 0.109375
- small: float32 [215, 768], P(None, 'fsdp'), may hold values from -4 to 4
- muon_square: float32 [3, 768, 768], P(None, 'fsdp'), may hold values from -0.0009765625 to 0.0009765625
- muon_qkv: float32 [768, 2304], P('fsdp'), may hold values from -0.0009765625 to 0.0009765625
- muon_up: float32 [768, 3072], P('fsdp'), may hold values from -0.0009765625 to 0.0009765625
- muon_down: float32 [3072, 768], P(None, 'fsdp'), may hold values from -0.0009765625 to 0.0009765625
- adam_first: float32 [215, 768], P(None, 'fsdp'), may hold values from -0.00061035156 to 0.00061035156
- adam_second: float32 [215, 768], P(None, 'fsdp'), may hold values from 5e-10 to 8e-09
Outputs:
- loss_sum: float32 [], replicated
- mask_count: float32 [], replicated
- grad_norm: float32 [], replicated
- new_square: float32 [3, 768, 768], P(None, 'fsdp')
- new_muon_square: float32 [3, 768, 768], P(None, 'fsdp')
- new_qkv: float32 [768, 2304], P('fsdp')
- new_muon_qkv: float32 [768, 2304], P('fsdp')
- new_up: float32 [768, 3072], P('fsdp')
- new_muon_up: float32 [768, 3072], P('fsdp')
- new_down: float32 [3072, 768], P(None, 'fsdp')
- new_muon_down: float32 [3072, 768], P(None, 'fsdp')
- new_small: float32 [215, 768], P(None, 'fsdp')
- new_first: float32 [215, 768], P(None, 'fsdp')
- new_second: float32 [215, 768], P(None, 'fsdp')
The draws below stay inside these ranges and needn't reach their ends.
All inputs are finite; a program needn't handle non-finite values.
Results may differ from the reference program's by a relative error of at most 0.01225.
The reference program's roundings to bfloat16 on the way count: a program that leaves them out, or rounds other values in their place, can miss the bound.
Values may be sent and summed in bfloat16 or wider, within the bound.
No kernel may reach another device: no remote copies, remote signals or barrier semaphores. Data moves between devices by JAX's collectives and lax.ppermute only.
A program may use at most 192 MiB of HBM per device.

```python
import math
import jax
import jax.numpy as jnp
from jax import lax

D = 768
FF = 3072
HEADS = 12
HEAD_DIM = 64
GRID = 24
SHORT_GRID = 14
IMG_DEV = 1
NS_ITERS = 5
STEP = 10
PATCHES = 576
SHORT_PATCHES = 196
SEQ = 577
POS = 197
SMALL_ROWS = 215
IMAGES = 32


def draw_masks(key, part):
    key = jax.random.fold_in(key, 11)
    picks = jax.random.randint(key, (IMAGES, PATCHES), 0, 1000)
    image_index = jnp.arange(IMAGES, dtype=jnp.int32)
    limits = 150 + 500 * image_index // IMAGES
    return (picks < limits[:, None]).astype(jnp.int32)


def draw_small(key, part):
    key = jax.random.fold_in(key, 23)
    row_total = 14 + FF // D + SHORT_GRID * SHORT_GRID + 1
    noise_key, factor_key = jax.random.split(key)
    noise = jnp.clip(jax.random.normal(noise_key, (row_total, D), jnp.float32), -4.0, 4.0)
    ramp_start = 0.5
    factor = jax.random.uniform(factor_key, (row_total, D), jnp.float32, 0.8, 1.2)
    column = jnp.arange(D, dtype=jnp.float32) / (D - 1)
    ramp = (ramp_start + column)[None, :] * factor
    row_index = jnp.arange(row_total)[:, None]
    is_gain = (row_index == 3) | (row_index == 6) | (row_index == 9)
    row_scale = jnp.where(row_index < 3, jnp.where(row_index == 0, 0.3, 1.0), jnp.where(row_index >= 14 + FF // D, 0.5, 0.3))
    return jnp.where(is_gain, ramp, noise * row_scale)


def plant(drawn, rng, smallest, top_value):
    longest = drawn.shape.index(max(drawn.shape))
    spots = []
    for shift in (0, 1):
        where = [jax.random.randint(jax.random.fold_in(rng, axis), (), 0, length) for axis, length in enumerate(drawn.shape)]
        where[longest] = (where[longest] + shift) % drawn.shape[longest]
        spots.append(tuple(where))
    return drawn.at[spots[0]].set(smallest).at[spots[1]].set(top_value)


def shard_levels(stream_key, extent, shards, smallest, high):
    loudness = 1.0
    for dim, parts in shards:
        heights = jax.random.uniform(jax.random.fold_in(jax.random.fold_in(stream_key, 6), dim), (parts,), jnp.float32, smallest / len(shards), high / len(shards))
        loudness = loudness * jnp.repeat(jnp.exp(heights), extent[dim] // parts).reshape((-1,) + (1,) * (len(extent) - 1 - dim))
    return loudness


def scatter_about(own_key, extent, scale, reach, pieces=(), kind=jnp.bfloat16):
    loudness = shard_levels(own_key, extent, pieces, -0.22, 0.18) if pieces else 1.0
    array = jax.random.normal(own_key, extent, jnp.float32) * scale * loudness
    return jnp.minimum(jnp.maximum(array, -reach), reach).astype(kind)


def setup_inputs(seed: int = 0) -> dict:
    arg_keys = jax.random.split(jax.random.key(seed), 15)
    return {
        "patches": scatter_about(arg_keys[0], (IMAGES, PATCHES, D), 1.0, 6.0, ((0, 32),)),
        "masks": draw_masks(jax.random.fold_in(arg_keys[14], 71), 0),
        "groups": plant(jax.random.randint(arg_keys[2], (IMAGES,), 0, 2), jax.random.fold_in(arg_keys[2], 1), 0, 1).astype(jnp.int32),
        "w_square": scatter_about(arg_keys[3], (3, D, D), 0.08, 0.5, ((1, 16),), jnp.float32),
        "w_qkv": scatter_about(arg_keys[4], (D, 3 * D), D ** -0.5, 0.21875, ((0, 16),), jnp.float32),
        "w_up": scatter_about(arg_keys[5], (D, FF), D ** -0.5, 0.21875, ((0, 16),), jnp.float32),
        "w_down": scatter_about(arg_keys[6], (FF, D), FF ** -0.5, 0.109375, ((1, 16),), jnp.float32),
        "small": draw_small(jax.random.fold_in(arg_keys[14], 71), 0),
        "muon_square": scatter_about(arg_keys[8], (3, D, D), (1.7e-4), 0.0009765625, ((1, 16),), jnp.float32),
        "muon_qkv": scatter_about(arg_keys[9], (D, 3 * D), (1.7e-4), 0.0009765625, ((0, 16),), jnp.float32),
        "muon_up": scatter_about(arg_keys[10], (D, FF), (1.7e-4), 0.0009765625, ((0, 16),), jnp.float32),
        "muon_down": scatter_about(arg_keys[11], (FF, D), (1.7e-4), 0.0009765625, ((1, 16),), jnp.float32),
        "adam_first": scatter_about(arg_keys[12], (SMALL_ROWS, D), (1.1e-4), 0.00061035156, ((1, 16),), jnp.float32),
        "adam_second": jnp.clip(jnp.exp(math.log(7.999999773744548e-09) - 2.7725887 * jax.random.uniform(arg_keys[13], (SMALL_ROWS, D), jnp.float32) ** shard_levels(arg_keys[13], (SMALL_ROWS, D), ((1, 16),), -0.2, 0.2)), 4.999999858590343e-10, 7.999999773744548e-09),
    }


@jax.custom_vjp
def low(v):
    return lax.optimization_barrier(v.astype(jnp.bfloat16)).astype(jnp.float32)

@jax.custom_vjp
def low_back(v):
    return v

def low_keep(v):
    return (low(v), None)

def low_pass(kept, grad):
    return (grad,)

def back_keep(v):
    return (v, None)

def back_low(kept, grad):
    return (low(grad),)
low.defvjp(low_keep, low_pass)
low_back.defvjp(back_keep, back_low)
layer_eps = 1e-06
coeff_first, coeff_second, coeff_third = (3.4445, -4.775, 2.0315)
momentum_decay = 0.95
muon_rate = 0.15
muon_decay = 0.01
beta_first = 0.9
beta_second = 0.999
adam_rate = 0.3
adam_eps = 1e-08
clip_limit = 0.5
masked_score = -1000000000.0

def interp_table(grid_side, short_side):
    axis_rows = []
    for target in range(grid_side):
        source = (target + 0.5) * short_side / grid_side - 0.5
        source = min(max(source, 0.0), short_side - 1.0)
        below = int(math.floor(source))
        above = min(below + 1, short_side - 1)
        upper_weight = source - below
        table_row = [0.0] * short_side
        table_row[below] += 1.0 - upper_weight
        table_row[above] += upper_weight
        axis_rows.append(table_row)
    axis_table = jnp.asarray(axis_rows, dtype=jnp.float32)
    lookup = jnp.zeros((1 + grid_side * grid_side, 1 + short_side * short_side), jnp.float32)
    lookup = lookup.at[0, 0].set(1.0)
    return lookup.at[1:, 1:].set(jnp.kron(axis_table, axis_table))

def layer_norm(values, gain, shift):
    centred = values - lax.optimization_barrier(jnp.mean(values, axis=-1, keepdims=True))
    variance = lax.optimization_barrier(jnp.mean(centred * centred, axis=-1, keepdims=True))
    return centred * lax.rsqrt(variance + layer_eps) * gain + shift

def highest(left, right):
    return jnp.matmul(left, right, precision=lax.Precision.HIGHEST)

def rounded(values):
    return lax.optimization_barrier(values.astype(jnp.bfloat16))

def orthogonalize(sent):
    widened = sent.astype(jnp.float32)
    frob_norm = jnp.sqrt(jnp.sum(widened * widened))
    current = rounded(widened / (frob_norm + 1e-07))
    for sweep in range(NS_ITERS):
        gram_low = rounded(jnp.dot(current, current.T, preferred_element_type=jnp.float32))
        poly_low = rounded(coeff_second * gram_low.astype(jnp.float32) + coeff_third * jnp.dot(gram_low, gram_low, preferred_element_type=jnp.float32))
        current = rounded(coeff_first * current.astype(jnp.float32) + jnp.dot(poly_low, current, preferred_element_type=jnp.float32))
    return current

def batch_loss(params, patch_batch, chosen, long_rows, lookup):
    square, qkv_weight, up_weight, down_weight, small_low = [low(item) for item in params]
    image_count = patch_batch.shape[0]
    up_rows = FF // D
    embedded = low_back(highest(patch_batch, square[0])) + small_low[0]
    embedded = jnp.where(chosen[..., None], small_low[1], embedded)
    leading = jnp.broadcast_to(small_low[2], (image_count, 1, D))
    position = small_low[14 + up_rows:]
    long_pos = highest(lookup, position)
    short_pos = jnp.pad(position, ((0, SEQ - POS), (0, 0)))
    resid = jnp.concatenate([leading, embedded], axis=1) + jnp.where(long_rows[:, None, None], long_pos, short_pos)
    key_limit = jnp.where(long_rows, SEQ, POS)
    key_valid = jnp.arange(SEQ)[None, :] < key_limit[:, None]
    normed = low(layer_norm(resid, small_low[3], small_low[4]))
    zero_row = jnp.zeros((D,), jnp.float32)
    mixed = low_back(highest(normed, qkv_weight)) + jnp.concatenate([small_low[12], zero_row, small_low[13]])
    heads_shape = (image_count, SEQ, HEADS, HEAD_DIM)
    query_rows = low(mixed[..., :D]).reshape(heads_shape)
    key_rows = low(mixed[..., D:2 * D]).reshape(heads_shape)
    value_rows = low(mixed[..., 2 * D:]).reshape(heads_shape)
    scores = low_back(jnp.einsum('iqhd,ikhd->ihqk', query_rows, key_rows, precision=lax.Precision.HIGHEST)) * HEAD_DIM ** (-0.5)
    scores = jnp.where(key_valid[:, None, None, :], scores, masked_score)
    expo = jnp.exp(scores - lax.optimization_barrier(jnp.max(scores, axis=-1, keepdims=True)))
    probs = expo / lax.optimization_barrier(jnp.sum(expo, axis=-1, keepdims=True))
    context = low_back(jnp.einsum('ihqk,ikhd->iqhd', low(probs), value_rows, precision=lax.Precision.HIGHEST)).reshape(image_count, SEQ, D)
    resid = resid + low_back(highest(low(context), square[1])) + small_low[5]
    normed = low(layer_norm(resid, small_low[6], small_low[7]))
    hidden_pre = low_back(highest(normed, up_weight)) + small_low[14:14 + up_rows].reshape(FF)
    activ = low(jax.nn.gelu(hidden_pre, approximate=False))
    resid = resid + low_back(highest(activ, down_weight)) + small_low[8]
    normed = low(layer_norm(resid, small_low[9], small_low[10]))
    predicted = low_back(highest(normed[:, 1:], square[2])) + small_low[11]
    residual_error = predicted - patch_batch
    return jnp.sum(jnp.where(chosen[..., None], residual_error * residual_error, 0.0))

def reference(patches, masks, groups, w_square, w_qkv, w_up, w_down, small, muon_square, muon_qkv, muon_up, muon_down, adam_first, adam_second):
    long_rows = groups > 0
    patch_limit = jnp.where(long_rows, PATCHES, SHORT_PATCHES)
    chosen = (masks > 0) & (jnp.arange(PATCHES)[None, :] < patch_limit[:, None])
    mask_count = jnp.sum(chosen.astype(jnp.float32))
    lookup = interp_table(GRID, SHORT_GRID)
    params = (w_square, w_qkv, w_up, w_down, small)
    batches = IMAGES // IMG_DEV
    data = (patches.astype(jnp.float32).reshape(batches, IMG_DEV, PATCHES, D), chosen.reshape(batches, IMG_DEV, PATCHES), long_rows.reshape(batches, IMG_DEV))

    def accumulate(carry, batch):
        totals, loss_total = carry
        patch_batch, chosen_batch, long_batch = batch
        loss_value, pullback = jax.vjp(lambda *items: batch_loss(items, patch_batch, chosen_batch, long_batch, lookup), *params)
        grads = pullback(jnp.ones((), jnp.float32) / mask_count)
        return ((tuple((left + right for left, right in zip(totals, grads))), loss_total + loss_value), None)
    start = (tuple((jnp.zeros_like(item) for item in params)), jnp.zeros((), jnp.float32))
    (grads, loss_sum), unused = lax.scan(accumulate, start, data)
    grad_norm = jnp.sqrt(sum((jnp.sum(item * item) for item in grads)))
    factor = jnp.minimum(1.0, clip_limit / (grad_norm + 1e-06))
    clipped = [item * factor for item in grads]
    weight_views = [w_square[0], w_square[1], w_square[2], w_qkv, w_up, w_down.T]
    moment_views = [muon_square[0], muon_square[1], muon_square[2], muon_qkv, muon_up, muon_down.T]
    grad_views = [clipped[0][0], clipped[0][1], clipped[0][2], clipped[1], clipped[2], clipped[3].T]
    new_weights, new_moments = ([], [])
    for weight, moment, gradient in zip(weight_views, moment_views, grad_views):
        moment_new = momentum_decay * moment + gradient
        blend = gradient + momentum_decay * moment_new
        ortho = orthogonalize(rounded(blend)).astype(jnp.float32)
        columns = weight.shape[1]
        new_weights.append(weight * (1.0 - muon_rate * muon_decay) - muon_rate * 0.2 * math.sqrt(columns) * ortho)
        new_moments.append(moment_new)
    grad_small = clipped[4]
    new_first = beta_first * adam_first + (1.0 - beta_first) * grad_small
    new_second = beta_second * adam_second + (1.0 - beta_second) * grad_small * grad_small
    first_hat = new_first / (1.0 - beta_first ** STEP)
    second_hat = new_second / (1.0 - beta_second ** STEP)
    new_small = small - adam_rate * first_hat / (jnp.sqrt(second_hat) + adam_eps)
    return (loss_sum, mask_count, grad_norm, jnp.stack(new_weights[:3]), jnp.stack(new_moments[:3]), new_weights[3], new_moments[3], new_weights[4], new_moments[4], new_weights[5].T, new_moments[5].T, new_small, new_first, new_second)
```

```python
from functools import partial
import math

import jax
import jax.numpy as jnp
import numpy as np
from jax import lax
from jax.experimental import pallas as pl
from jax.experimental.pallas import tpu as pltpu
from jax.sharding import PartitionSpec as P

D = 768
FF = 3072
HEADS = 12
HEAD_DIM = 64
GRID = 24
SHORT_GRID = 14
NS_ITERS = 5
STEP = 10
PATCHES = 576
SHORT_PATCHES = 196
UP_ROWS = FF // D
POS = SHORT_PATCHES + 1
SMALL_ROWS = 14 + UP_ROWS + POS
CLASS_ROW = PATCHES
TOKENS = 592
SMALL_PAD = 256
MIB = 1024 * 1024
SCALE = HEAD_DIM**-0.5

layer_eps = 1e-06
coeff_first, coeff_second, coeff_third = (3.4445, -4.775, 2.0315)
momentum_decay = 0.95
muon_rate = 0.15
muon_decay = 0.01
beta_first = 0.9
beta_second = 0.999
adam_rate = 0.3
adam_eps = 1e-08
clip_limit = 0.5
masked_score = -1000000000.0

BOTH = ("fsdp", "dp")
bfloat = jnp.bfloat16
float32 = jnp.float32


def interp_tables():
    axis_table = np.zeros((GRID, SHORT_GRID), np.float64)
    for target in range(GRID):
        source = (target + 0.5) * SHORT_GRID / GRID - 0.5
        source = min(max(source, 0.0), SHORT_GRID - 1.0)
        below = int(math.floor(source))
        above = min(below + 1, SHORT_GRID - 1)
        axis_table[target, below] += 1.0 - (source - below)
        axis_table[target, above] += source - below
    axis_table = axis_table.astype(np.float32)
    long_table = np.zeros((TOKENS, POS), np.float32)
    long_table[:PATCHES, 1:] = np.kron(axis_table, axis_table)
    long_table[CLASS_ROW, 0] = 1.0
    short_table = np.zeros((TOKENS, POS), np.float32)
    short_table[:SHORT_PATCHES, 1:] = np.eye(SHORT_PATCHES)
    short_table[CLASS_ROW, 0] = 1.0
    return long_table, short_table


def cost(flops, bytes_accessed, transcendentals):
    return pl.CostEstimate(
        flops=flops, bytes_accessed=bytes_accessed, transcendentals=0
    )


def dot_nt(left, right):
    return lax.dot_general(left, right, (((1,), (1,)), ((), ())), preferred_element_type=float32)


def dot_nn(left, right):
    return lax.dot_general(left, right, (((1,), (0,)), ((), ())), preferred_element_type=float32)


def dot_tn(left, right):
    return lax.dot_general(left, right, (((0,), (0,)), ((), ())), preferred_element_type=float32)


def attend_forward_kernel(q_ref, k_ref, v_ref, keep_ref, context_ref, logsum_ref):
    keep = keep_ref[...] > 0
    outs = []
    for head in range(2):
        cols = slice(HEAD_DIM * head, HEAD_DIM * (head + 1))
        query, key, value = q_ref[:, cols] * SCALE, k_ref[:, cols], v_ref[:, cols]
        scores = jnp.where(keep, dot_nt(key, query), masked_score)
        peak = jnp.max(scores, axis=0, keepdims=True)
        expo = jnp.exp(scores - peak)
        total = jnp.sum(expo, axis=0, keepdims=True)
        probs = (expo * (1.0 / total)).astype(bfloat)
        outs.append(dot_nn(value.T, probs).T.astype(bfloat))
        logsum_ref[head] = peak + jnp.log(total)
    context_ref[...] = jnp.concatenate(outs, axis=1)


def attend_backward_kernel(
    place_ref, q_ref, k_ref, v_ref, grad_ref, logsum_ref, keep_ref, mixed_ref, sums_ref
):
    keep = keep_ref[...] > 0
    grads_query, grads_key, grads_value = [], [], []
    for head in range(2):
        cols = slice(HEAD_DIM * head, HEAD_DIM * (head + 1))
        query, key, value, grad = q_ref[:, cols], k_ref[:, cols], v_ref[:, cols], grad_ref[:, cols]
        query, scaled_key = query * SCALE, key * SCALE
        scores = dot_nt(key, query)
        probs = jnp.where(keep, jnp.exp(scores - logsum_ref[head]), 0.0)
        grad_probs = dot_nt(value, grad)
        grads_value.append(dot_nn(probs.astype(bfloat), grad))
        mixed = probs * grad_probs
        total = jnp.sum(mixed, axis=0, keepdims=True)
        scores_low = (mixed - probs * total).astype(bfloat)
        grads_key.append(dot_nn(scores_low, query))
        grads_query.append(dot_nn(scaled_key.T, scores_low).T)
    grad_query = jnp.concatenate(grads_query, axis=1)
    grad_value = jnp.concatenate(grads_value, axis=1)
    mixed_ref[0] = grad_query.astype(bfloat)
    mixed_ref[1] = jnp.concatenate(grads_key, axis=1).astype(bfloat)
    mixed_ref[2] = grad_value.astype(bfloat)
    sums_ref[0:1, :] = jnp.sum(grad_query, axis=0, keepdims=True)
    sums_ref[1:2, :] = jnp.sum(grad_value, axis=0, keepdims=True)


def head_block(offset):
    return pl.BlockSpec((TOKENS, 2 * HEAD_DIM), lambda pair: (0, offset + pair))


KEEP_BLOCK = pl.BlockSpec((TOKENS, 1), lambda pair: (0, 0))
LOGSUM_BLOCK = pl.BlockSpec((2, 1, TOKENS), lambda pair: (pair, 0, 0))
PAIRS = HEADS // 2


def attend_forward(mixed, keep):
    return pl.pallas_call(
        attend_forward_kernel,
        grid=(PAIRS,),
        in_specs=[head_block(0), head_block(PAIRS), head_block(2 * PAIRS), KEEP_BLOCK],
        out_specs=[head_block(0), LOGSUM_BLOCK],
        out_shape=[
            jax.ShapeDtypeStruct((TOKENS, D), bfloat),
            jax.ShapeDtypeStruct((HEADS, 1, TOKENS), float32),
        ],
        cost_estimate=cost(
            flops=8 * TOKENS * TOKENS * D, bytes_accessed=8 * TOKENS * D, transcendentals=0
        ),
        compiler_params=pltpu.CompilerParams(vmem_limit_bytes=24 * MIB),
    )(mixed, mixed, mixed, keep)


def attend_backward(mixed, grad, logsum, keep, part, count):
    pairs = PAIRS // count
    lanes = 2 * HEAD_DIM

    def block(offset):
        return pl.BlockSpec((TOKENS, lanes), lambda pair, place: (0, offset + place[0] * pairs + pair))

    return pl.pallas_call(
        attend_backward_kernel,
        grid_spec=pltpu.PrefetchScalarGridSpec(
            num_scalar_prefetch=1,
            grid=(pairs,),
            in_specs=[
                block(0),
                block(PAIRS),
                block(2 * PAIRS),
                block(0),
                pl.BlockSpec((2, 1, TOKENS), lambda pair, place: (place[0] * pairs + pair, 0, 0)),
                pl.BlockSpec((TOKENS, 1), lambda pair, place: (0, 0)),
            ],
            out_specs=[
                pl.BlockSpec((3, TOKENS, lanes), lambda pair, place: (0, 0, pair)),
                pl.BlockSpec((2, lanes), lambda pair, place: (0, pair)),
            ],
        ),
        out_shape=[
            jax.ShapeDtypeStruct((3, TOKENS, pairs * lanes), bfloat),
            jax.ShapeDtypeStruct((2, pairs * lanes), float32),
        ],
        cost_estimate=cost(
            flops=20 * TOKENS * TOKENS * pairs * lanes,
            bytes_accessed=16 * TOKENS * pairs * lanes,
            transcendentals=0,
        ),
        compiler_params=pltpu.CompilerParams(vmem_limit_bytes=28 * MIB),
    )(part.reshape(1).astype(jnp.int32), mixed, mixed, mixed, grad, logsum, keep)


def stack_kernel(*refs):
    out_ref, start = refs[-1], 0
    for ref in refs[:-1]:
        out_ref[start : start + ref.shape[0], :] = ref[...]
        start += ref.shape[0]
    out_ref[start:, :] = jnp.zeros((out_ref.shape[0] - start, out_ref.shape[1]), out_ref.dtype)


def stacked_rows(parts, count):
    return pl.pallas_call(
        stack_kernel, out_shape=jax.ShapeDtypeStruct((count, parts[0].shape[1]), float32)
    )(*parts)


def gelu_parts(values):
    size = 1.0 + 0.23164189 * jnp.abs(values)
    inner = pl.reciprocal(size, approx=True)
    inner = inner * (2.0 - size * inner)
    poly = jnp.full_like(inner, 0.5 * 1.061405429)
    for coeff in (-1.453152027, 1.421413741, -0.284496736, 0.254829592):
        poly = poly * inner + 0.5 * coeff
    bell = jnp.exp(-0.5 * values * values)
    tail = poly * inner * bell
    below = jnp.where(values >= 0.0, 1.0 - tail, tail)
    return values * below, below + values * (0.3989422804014327 * bell)


UP_TILE = 768
UP_ROW_TILE = 160


def up_kernel(normed_ref, weight_ref, bias_ref, activ_ref, slope_ref):
    for start in range(0, TOKENS, UP_ROW_TILE):
        rows = slice(start, min(start + UP_ROW_TILE, TOKENS))
        hidden = dot_nn(normed_ref[rows], weight_ref[...]) + bias_ref[...]
        activ, slope = gelu_parts(hidden)
        activ_ref[rows] = activ.astype(bfloat)
        slope_ref[rows] = slope


def up_forward(normed, weight, bias):
    tile = pl.BlockSpec((TOKENS, UP_TILE), lambda step: (0, step))
    return pl.pallas_call(
        up_kernel,
        grid=(FF // UP_TILE,),
        in_specs=[
            pl.BlockSpec((TOKENS, D), lambda step: (0, 0)),
            pl.BlockSpec((D, UP_TILE), lambda step: (0, step)),
            pl.BlockSpec((1, UP_TILE), lambda step: (0, step)),
        ],
        out_specs=[tile, tile],
        out_shape=[
            jax.ShapeDtypeStruct((TOKENS, FF), bfloat),
            jax.ShapeDtypeStruct((TOKENS, FF), float32),
        ],
        cost_estimate=cost(
            flops=2 * TOKENS * D * FF, bytes_accessed=20 * MIB, transcendentals=0
        ),
        compiler_params=pltpu.CompilerParams(vmem_limit_bytes=20 * MIB),
    )(normed, weight, bias)


def hidden_kernel(branch_ref, weight_ref, slope_ref, hidden_ref, sums_ref):
    grad = dot_nn(branch_ref[...], weight_ref[...]) * slope_ref[...]
    hidden_ref[...] = grad.astype(bfloat)
    sums_ref[...] = jnp.sum(grad, axis=0, keepdims=True)


def hidden_backward(branch, weight, slope):
    tile = pl.BlockSpec((TOKENS, UP_TILE), lambda step: (0, step))
    return pl.pallas_call(
        hidden_kernel,
        grid=(FF // UP_TILE,),
        in_specs=[
            pl.BlockSpec((TOKENS, D), lambda step: (0, 0)),
            pl.BlockSpec((D, UP_TILE), lambda step: (0, step)),
            tile,
        ],
        out_specs=[tile, pl.BlockSpec((1, UP_TILE), lambda step: (0, step))],
        out_shape=[
            jax.ShapeDtypeStruct((TOKENS, FF), bfloat),
            jax.ShapeDtypeStruct((1, FF), float32),
        ],
        cost_estimate=cost(
            flops=2 * TOKENS * D * FF, bytes_accessed=20 * MIB, transcendentals=0
        ),
        compiler_params=pltpu.CompilerParams(vmem_limit_bytes=20 * MIB),
    )(branch, weight, slope)


def normalized(values):
    centred = values - jnp.mean(values, axis=-1, keepdims=True)
    variance = jnp.mean(centred * centred, axis=-1, keepdims=True)
    inverse = lax.rsqrt(variance + layer_eps)
    return centred * inverse, inverse


def norm_backward(grad, unit, inverse, gain):
    grad_unit = grad * gain
    mean_grad = jnp.mean(grad_unit, axis=-1, keepdims=True)
    mean_mixed = jnp.mean(grad_unit * unit, axis=-1, keepdims=True)
    grad_values = inverse * (grad_unit - mean_grad - unit * mean_mixed)
    return (
        grad_values,
        jnp.sum(grad * unit, axis=0, keepdims=True),
        jnp.sum(grad, axis=0, keepdims=True),
    )


TILE = 256


def ortho_kernel(squares_ref, own_ref, other_ref, out_ref, full_ref, gram_ref, poly_ref, *, places, shares, stride):
    rows, share = own_ref.shape[1], own_ref.shape[2]
    own_rows = out_ref.shape[0]
    width = shares * stride

    def pieces():
        for core, ref in enumerate((own_ref, other_ref)):
            for place in range(places):
                for part in range(2):
                    for column in range(shares):
                        index = place * shares + column if part == 0 else column * places + place
                        top = core * (D // 2) + (2 * place + part) * rows
                        yield ref, part * places * shares + index, top, column

    def inverse_norm(total):
        return 1.0 / (jnp.sqrt(total) + 1e-07)

    def mirrored(ref, make):
        for i in range(D // TILE):
            ref[i * TILE : (i + 1) * TILE, : (i + 1) * TILE] = make(i).astype(bfloat)
            for j in range(i):
                block = ref[i * TILE : (i + 1) * TILE, j * TILE : (j + 1) * TILE]
                ref[j * TILE : (j + 1) * TILE, i * TILE : (i + 1) * TILE] = block.T

    def grams(start, columns):
        def gram(i):
            return dot_nt(
                full_ref[i * TILE : (i + 1) * TILE, pl.ds(start, columns)],
                full_ref[: (i + 1) * TILE, pl.ds(start, columns)],
            )

        def poly(i):
            block = gram_ref[i * TILE : (i + 1) * TILE, :]
            product = dot_nn(block, gram_ref[:, : (i + 1) * TILE])
            return coeff_second * block[:, : (i + 1) * TILE].astype(float32) + coeff_third * product

        mirrored(gram_ref, gram)
        mirrored(poly_ref, poly)

    def step(start, columns, tall, target):
        old = full_ref[:, pl.ds(start, columns)]
        fresh = coeff_first * old[:tall].astype(float32) + dot_nn(poly_ref[:tall, :], old)
        target[:tall, pl.ds(start, columns)] = fresh.astype(bfloat)

    @pl.when(squares_ref[0] == 0)
    def one_matrix():
        total = jnp.zeros((), float32)
        for ref in (own_ref, other_ref):
            for index in range(ref.shape[0]):
                values = ref[index].astype(float32)
                total = total + jnp.sum(values * values)
        scale = inverse_norm(total)
        for ref, index, top, column in pieces():
            full_ref[top : top + rows, column * share : (column + 1) * share] = (
                ref[index].astype(float32) * scale
            ).astype(bfloat)
        columns = shares * share

        @pl.loop(0, NS_ITERS - 1)
        def sweep(index):
            grams(0, columns)
            step(0, columns, D, full_ref)

        grams(0, columns)
        step(0, columns, own_rows, out_ref)

    @pl.when(squares_ref[0] != 0)
    def three_matrices():
        for square in range(3):
            part = slice(square * stride, (square + 1) * stride)
            total = jnp.zeros((), float32)
            for ref in (own_ref, other_ref):
                for index in range(ref.shape[0]):
                    values = ref[index, :, part].astype(float32)
                    total = total + jnp.sum(values * values)
            scale = inverse_norm(total)
            for ref, index, top, column in pieces():
                left = square * width + column * stride
                full_ref[top : top + rows, left : left + stride] = (
                    ref[index, :, part].astype(float32) * scale
                ).astype(bfloat)

        @pl.loop(0, 3)
        def one(square):
            start = pl.multiple_of(square * width, 128)

            @pl.loop(0, NS_ITERS - 1)
            def sweep(index):
                grams(start, width)
                step(start, width, D, full_ref)

            grams(start, width)
            step(start, width, own_rows, out_ref)


def orthogonalize(squares, own, other, places, shares, stride, own_rows):
    count, rows, share = own.shape
    columns = max(shares * share, 3 * shares * stride)
    return pl.pallas_call(
        partial(ortho_kernel, places=places, shares=shares, stride=stride),
        in_specs=[
            pl.BlockSpec(memory_space=pltpu.SMEM),
            pl.BlockSpec(memory_space=pltpu.VMEM),
            pl.BlockSpec(memory_space=pltpu.VMEM),
        ],
        out_specs=pl.BlockSpec(memory_space=pltpu.VMEM),
        out_shape=jax.ShapeDtypeStruct((own_rows, columns), bfloat),
        scratch_shapes=[
            pltpu.VMEM((D, columns), bfloat),
            pltpu.VMEM((D, D), bfloat),
            pltpu.VMEM((D, D), bfloat),
        ],
        cost_estimate=cost(
            flops=10 * D * D * (2 * FF + D), bytes_accessed=8 * MIB, transcendentals=0
        ),
        compiler_params=pltpu.CompilerParams(vmem_limit_bytes=44 * MIB),
    )(squares, own, other)


class Wires:
    def __init__(self):
        self.fsdp_size, self.dp_size = lax.axis_size("fsdp"), lax.axis_size("dp")
        self.count = self.fsdp_size * self.dp_size
        self.fsdp, self.dp = lax.axis_index("fsdp"), lax.axis_index("dp")
        self.me = self.fsdp * self.dp_size + self.dp
        dp_bits = self.dp_size.bit_length() - 1
        all_bits = self.count.bit_length() - 1
        assert self.count == 1 << all_bits and self.fsdp_size >= 8
        self.dp_bits = list(range(dp_bits))
        self.core_bit = dp_bits
        self.row_bits = list(range(dp_bits + 1, all_bits - 2))
        self.near_bit, self.far_bit = all_bits - 2, all_bits - 1
        self.all_bits = list(range(all_bits))
        self.group = self.me >> self.near_bit

    def bit(self, bit):
        return (self.me >> bit) & 1

    def swap(self, values, bit):
        return self.swap_mask(values, 1 << bit)

    def swap_mask(self, values, mask):
        return lax.ppermute(values, BOTH, [(i, i ^ mask) for i in range(self.count)])

    def total(self, values):
        for bit in [self.core_bit] + self.dp_bits + self.row_bits + [self.near_bit, self.far_bit]:
            values = values + self.swap(values, bit)
        return values


def after(values, *others):
    return lax.optimization_barrier((values,) + others)[0]


def together(*values):
    return lax.optimization_barrier(values)


def split_exact(values):
    high = values.astype(bfloat)
    return jnp.concatenate([high, (values - high.astype(float32)).astype(bfloat)], axis=-1)


def joined_exact(sent):
    width = sent.shape[-1] // 2
    return sent[..., :width].astype(float32) + sent[..., width:].astype(float32)


def own_selection(wires):
    low = wires.fsdp_size // 4
    block = D // wires.fsdp_size
    place = jnp.arange(D // 2)
    distance, group, inner = place // (4 * block), place // block % 4, place % block
    count = len(wires.row_bits)
    flips = sum(
        ((distance >> (count - 1 - i)) & 1) << (bit - wires.core_bit)
        for i, bit in enumerate(wires.row_bits)
    )
    source = (group * low + ((wires.fsdp % low) ^ flips)) * block + inner
    return (source[:, None] == jnp.arange(D)[None, :]).astype(bfloat)


def pair_kernel(
    place_ref, select_ref, left_ref, left_other_ref, right_ref, right_other_ref,
    near_ref, away_ref, rows_ref, rows_other_ref, *, by_rows, halves
):
    @pl.when((pl.program_id(0) == 0) & (pl.program_id(1) == 0) & (pl.program_id(2) == 0))
    def select():
        rows_ref[...] = dot_nt(select_ref[...], left_ref[...]).astype(bfloat)
        rows_other_ref[...] = dot_nt(select_ref[...], left_other_ref[...]).astype(bfloat)

    right = right_ref[...].reshape(right_ref.shape[-2:])
    right_other = right_other_ref[...].reshape(right.shape)
    product = dot_nn(rows_ref[...], right) + dot_nn(rows_other_ref[...], right_other)
    if by_rows:
        half = product.shape[0] // 2
        near_ref[0, 0] = product[:half]
        away_ref[0, 0] = product[half:].astype(bfloat)
    else:

        @pl.when(pl.program_id(0) < halves)
        def away():
            away_ref[0, 0] = product.astype(bfloat)

        @pl.when(pl.program_id(0) >= halves)
        def near():
            near_ref[0, 0] = product


def column_tiles(width, cuts):
    sizes = [size for size in (768, 512, 384, 256, 128) if width % size == 0 and width // size >= cuts]
    return sizes[0] if sizes else width


def pair_grad(wires, select, left, right, by_rows, parts=None, cut=None):
    left, left_other = left
    right, right_other = right
    tokens, columns = right.shape[1:]
    first_part, parts = (0, right.shape[0]) if parts is None else parts
    dp_size = wires.dp_size
    width = columns // dp_size
    halves = dp_size // 2
    tile = column_tiles(width, 1 if cut is None else 2)
    all_steps = width // tile
    first_step, steps = 0, all_steps
    if cut is not None:
        edge = all_steps // 2
        first_step, steps = (0, edge) if cut == 0 else (edge, all_steps - edge)
    if tile % 128:
        right, right_other = (
            item.reshape(item.shape[0], tokens, dp_size, width).transpose(2, 0, 1, 3)
            for item in (right, right_other)
        )

    def distance(turn):
        return turn if by_rows else jnp.where(turn < halves, 2 * turn + 1, 2 * (turn - halves))

    def right_place(turn, part, step, place):
        column = distance(turn) ^ place[0]
        if right.ndim == 4:
            return (column, first_part + part, 0, 0)
        return (first_part + part, 0, column * all_steps + first_step + step)

    right_block = (1, 1, tokens, width) if right.ndim == 4 else (1, tokens, tile)
    rows = D // 2
    if by_rows:
        rows //= 2
        count = dp_size

        def near_place(turn, part, step, place):
            return (turn, part, 0, step)

        away_place = near_place
    else:
        count = halves

        def near_place(turn, part, step, place):
            there = turn >= halves
            return (
                jnp.maximum(turn - halves, 0),
                jnp.where(there, part, 0),
                0,
                jnp.where(there, step, 0),
            )

        def away_place(turn, part, step, place):
            there = turn < halves
            return (
                jnp.minimum(turn, halves - 1),
                jnp.where(there, part, parts - 1),
                0,
                jnp.where(there, step, steps - 1),
            )

    whole = pl.BlockSpec((tokens, D), lambda turn, part, step, place: (0, 0))
    shape = (count, parts, rows, steps * tile)
    return pl.pallas_call(
        partial(pair_kernel, by_rows=by_rows, halves=halves),
        grid_spec=pltpu.PrefetchScalarGridSpec(
            num_scalar_prefetch=1,
            grid=(dp_size, parts, steps),
            in_specs=[
                pl.BlockSpec((D // 2, D), lambda turn, part, step, place: (0, 0)),
                whole,
                whole,
                pl.BlockSpec(right_block, right_place),
                pl.BlockSpec(right_block, right_place),
            ],
            out_specs=[
                pl.BlockSpec((1, 1, rows, tile), near_place),
                pl.BlockSpec((1, 1, rows, tile), away_place),
            ],
            scratch_shapes=[pltpu.VMEM((D // 2, tokens), bfloat)] * 2,
        ),
        out_shape=[
            jax.ShapeDtypeStruct(shape, float32),
            jax.ShapeDtypeStruct(shape, bfloat),
        ],
        cost_estimate=cost(
            flops=2 * tokens * D * dp_size * steps * tile * parts,
            bytes_accessed=4 * D * dp_size * steps * tile * parts,
            transcendentals=0,
        ),
        compiler_params=pltpu.CompilerParams(vmem_limit_bytes=14 * MIB),
    )(wires.dp.reshape(1).astype(jnp.int32), select, left, left_other, right, right_other)


def product_kernel(select_ref, left_ref, left_other_ref, right_ref, right_other_ref, out_ref):
    rows = dot_nt(select_ref[...], left_ref[...]).astype(bfloat)
    rows_other = dot_nt(select_ref[...], left_other_ref[...]).astype(bfloat)
    width = right_ref.shape[-1]
    for part in range(right_ref.shape[0]):
        product = dot_nn(rows, right_ref[part]) + dot_nn(rows_other, right_other_ref[part])
        out_ref[:, part * width : (part + 1) * width] = product.astype(out_ref.dtype)


def pair_product(select, left, right, kind):
    parts, tokens, width = right[0].shape
    return pl.pallas_call(
        product_kernel,
        out_shape=jax.ShapeDtypeStruct((select.shape[0], parts * width), kind),
        cost_estimate=cost(
            flops=2 * tokens * D * parts * width, bytes_accessed=8 * MIB, transcendentals=0
        ),
        compiler_params=pltpu.CompilerParams(vmem_limit_bytes=16 * MIB),
    )(select, *left, *right)


def mixed_kernel(place_ref, away_ref, near_ref, weight_ref, out_ref):
    turn, part = pl.program_id(0), pl.program_id(1)

    @pl.when((turn == 0) & (part == 0))
    def start():
        out_ref[...] = jnp.zeros_like(out_ref)

    @pl.when(turn == 0)
    def away():
        out_ref[...] += dot_nt(away_ref[0], weight_ref[...])

    @pl.when(turn == 1)
    def near():
        out_ref[...] += dot_nt(near_ref[0], weight_ref[...])


def mixed_backward(place, away, near, weight):
    width = away.shape[-1]
    return pl.pallas_call(
        mixed_kernel,
        grid_spec=pltpu.PrefetchScalarGridSpec(
            num_scalar_prefetch=1,
            grid=(2, 3),
            in_specs=[
                pl.BlockSpec(
                    (1, TOKENS, width), lambda turn, part, place: (jnp.where(turn == 0, part, 2), 0, 0)
                ),
                pl.BlockSpec(
                    (1, TOKENS, width), lambda turn, part, place: (jnp.where(turn == 1, part, 0), 0, 0)
                ),
                pl.BlockSpec(
                    (D, width), lambda turn, part, place: (0, 2 * part + (place[0] ^ (1 - turn)))
                ),
            ],
            out_specs=pl.BlockSpec((TOKENS, D), lambda turn, part, place: (0, 0)),
        ),
        out_shape=jax.ShapeDtypeStruct((TOKENS, D), float32),
        cost_estimate=cost(
            flops=6 * TOKENS * D * D, bytes_accessed=10 * MIB, transcendentals=0
        ),
        compiler_params=pltpu.CompilerParams(vmem_limit_bytes=14 * MIB),
    )(place.reshape(1).astype(jnp.int32), away, near, weight)


def fold(values):
    distances, parts, rows, width = values.shape
    return values.transpose(0, 2, 1, 3).reshape(distances, rows, parts * width)


class Flow:
    def __init__(self, wires, plain, exact=None):
        self.wires, self.plain, self.exact, self.sent = wires, plain, exact, []

    @staticmethod
    def halves(values, by_rows):
        if by_rows:
            half = values.shape[1] // 2
            return values[:, :half], values[:, half:]
        values = values.reshape((values.shape[0] // 2, 2) + values.shape[1:])
        return values[:, 0], values[:, 1]

    def send(self, away, away_exact, bit):
        parts = [item.astype(bfloat) for item in away]
        if away_exact is not None:
            parts.append(split_exact(away_exact))
        self.sent.append(jnp.concatenate(parts, axis=-1) if len(parts) > 1 else parts[0])
        return self.wires.swap(self.sent[-1], bit)

    def halved(self, values, bit):
        return (None, None) if values is None else self.halves(values, bit in self.wires.row_bits)

    def finish(self, near, near_exact, got):
        start, sums = 0, []
        for item in near:
            width = item.shape[-1]
            sums.append(item + got[..., start : start + width].astype(float32))
            start += width
        exact = None if near_exact is None else near_exact + joined_exact(got[..., start:])
        return sums, exact

    def land(self, hold=()):
        pairs, near_exact, got = self.pending
        got = after(got, *hold) if hold else got
        self.plain, self.exact = self.finish([near for near, away in pairs], near_exact, got)
        return self

    def next(self, bit, hold=()):
        self.land(hold)
        by_rows = bit in self.wires.row_bits
        pairs = [self.halves(item, by_rows) for item in self.plain]
        near_exact, away_exact = self.halved(self.exact, bit)
        self.pending = (pairs, near_exact, self.send([away for near, away in pairs], away_exact, bit))
        return self

    def first(self, pairs, bit, exact=None):
        near_exact, away_exact = (
            (None, None) if exact is None else self.halves(exact, bit in self.wires.row_bits)
        )
        self.pending = (pairs, near_exact, self.send([away for near, away in pairs], away_exact, bit))
        return self


def gather_relative(wires, values, order):
    for bit in order:
        values = jnp.stack([values, wires.swap(values, bit)])
    return values


def dp_columns(wires, values):
    width = values.shape[-1] // wires.dp_size
    return lax.dynamic_slice_in_dim(values, wires.dp * width, width, values.ndim - 1)


def padded_to(values, width):
    pads = [(0, 0)] * (values.ndim - 1) + [(0, width - values.shape[-1])]
    return jnp.pad(values, pads)


def assemble_kernel(place_ref, *refs, pieces, count):
    outs, ins = refs[count:], refs[:count]
    row, core, dp = place_ref[0], place_ref[1], place_ref[2]
    for source, far_row, far_core, far_dp, start, matrix, offset, width in pieces:
        target = outs[matrix]
        part = target.shape[-1] // 2
        left = pl.multiple_of((dp ^ far_dp) * part + offset, 128)
        for group in range(4):
            target[group, row ^ far_row, core ^ far_core, :, pl.ds(left, width)] = ins[source[0]][
                source[1], group, :, start : start + width
            ]


def doubled(wires, values, bit, hold=()):
    got = wires.swap(values, bit)
    return jnp.stack([values, after(got, *hold) if hold else got])


def in_order(wires, values):
    return jnp.stack(
        [
            lax.dynamic_slice(
                values,
                ((group & 1) ^ wires.bit(wires.near_bit), (group >> 1) ^ wires.bit(wires.far_bit), 0, 0),
                (1, 1) + values.shape[2:],
            )[0, 0]
            for group in range(4)
        ]
    )


class Streams:
    def __init__(self, wires, along, widths, split):
        self.wires, self.widths, self.split = wires, widths, split
        edge = sum(widths[:-1]) + split
        self.first, self.last = along[..., :edge], along[..., edge:]

    def near(self, hold=()):
        wires = self.wires
        self.first = doubled(wires, self.first, wires.row_bits[0], hold)
        self.last = doubled(wires, self.last, wires.dp_bits[0], hold)

    def far(self, hold):
        self.first_far, self.last_far = together(self.first_far, self.last_far, *hold)[:2]

    def send_far(self):
        wires = self.wires
        self.first_far = wires.swap(self.first, wires.dp_bits[0])
        self.last_far = wires.swap(self.last, wires.row_bits[0])

    def finish(self):
        wires, widths, split = self.wires, self.widths, self.split
        block = self.first.shape[2]
        arrays = [
            jnp.concatenate([self.first, self.first_far]), jnp.concatenate([self.last, self.last_far])
        ]
        arrays += [wires.swap(item, wires.core_bit) for item in arrays]
        pieces = []
        for far_core in range(2):
            for far in range(2):
                for index in range(2):
                    start = 0
                    place = 2 * far + index
                    for matrix, width in enumerate(widths[:-1] + [split]):
                        source = (2 * far_core, place)
                        pieces.append((source, index, far_core, far, start, matrix, 0, width))
                        start += width
                    source = (2 * far_core + 1, place)
                    width = widths[-1] - split
                    pieces.append((source, far, far_core, index, 0, len(widths) - 1, split, width))
        place = jnp.stack(
            [wires.bit(wires.row_bits[0]), wires.bit(wires.core_bit), wires.bit(wires.dp_bits[0])]
        )
        wholes = pl.pallas_call(
            partial(assemble_kernel, pieces=pieces, count=len(arrays)),
            in_specs=[pl.BlockSpec(memory_space=pltpu.SMEM)]
            + [pl.BlockSpec(memory_space=pltpu.VMEM)] * len(arrays),
            out_specs=[pl.BlockSpec(memory_space=pltpu.VMEM)] * len(widths),
            out_shape=[
                jax.ShapeDtypeStruct((4, 2, 2, block, 2 * width), bfloat) for width in widths
            ],
            cost_estimate=cost(
                flops=0, bytes_accessed=4 * D * 2 * sum(widths), transcendentals=0
            ),
            compiler_params=pltpu.CompilerParams(vmem_limit_bytes=40 * MIB),
        )(place.astype(jnp.int32), *arrays)
        return [whole.reshape(D, whole.shape[-1]) for whole in wholes]


def side_by_side(parts, stride, width):
    return padded_to(jnp.concatenate([padded_to(part, stride) for part in parts], axis=-1), width)


def per_device(
    patches,
    masks,
    groups,
    w_square,
    w_qkv,
    w_up,
    w_down,
    small,
    muon_square,
    muon_qkv,
    muon_up,
    muon_down,
    adam_first,
    adam_second,
):
    wires = Wires()
    block = D // wires.fsdp_size
    dp_size = wires.dp_size

    long_image = groups[0] > 0
    patch_limit = jnp.where(long_image, PATCHES, SHORT_PATCHES)
    row = jnp.arange(TOKENS)
    chosen = jnp.pad(masks[0] > 0, (0, TOKENS - PATCHES)) & (row < patch_limit)
    chosen_float = chosen.astype(float32)[:, None]
    mask_local = jnp.sum(chosen_float)

    half = SMALL_PAD // 2
    used = -(-SMALL_ROWS // 2)
    small_low = small.astype(bfloat).T
    own_count = jnp.full((block, half - used), mask_local)
    high_count = jnp.floor(own_count / 256.0)
    lane = lax.broadcasted_iota(jnp.int32, own_count.shape, 1)
    spare = jnp.where(lane == 0, high_count, jnp.where(lane == 1, own_count - 256.0 * high_count, 0.0))
    spare = spare.astype(bfloat)
    small_rows = jnp.concatenate(
        [
            small_low[:, :used],
            spare,
            padded_to(small_low[:, used:], used),
            spare,
        ],
        axis=1,
    )
    square_low = w_square.astype(bfloat)
    down_rows = w_down.astype(bfloat).T
    groups_low = [
        [square_low[0], small_rows, w_qkv.astype(bfloat)],
        [square_low[1], w_up.astype(bfloat)],
        [square_low[2], down_rows],
    ]
    half_widths = [[shard.shape[1] // 2 for shard in shards] for shards in groups_low]
    staged = (
        dp_size == 2
        and len(wires.row_bits) == 1
        and not any(width % 128 for widths in half_widths for width in widths)
    )
    if staged:
        near_bit, far_bit = wires.near_bit, wires.far_bit

        def own_columns(shards):
            return jnp.concatenate([dp_columns(wires, shard) for shard in shards], axis=1)

        early_own, middle_own, late_own = [own_columns(shards) for shards in groups_low]
        early_own = doubled(wires, doubled(wires, early_own, far_bit), near_bit)
        early = Streams(wires, in_order(wires, early_own), half_widths[0], 256)
        middle_own = after(middle_own, early.first)
        early.near()
        early.send_far()
        middle_own = doubled(wires, middle_own, far_bit)
        early.far((middle_own,))
        embed_weight, small_whole, qkv_weight = early.finish()
        counts = small_whole.reshape(D, 2, half)[:, :, used : used + 2].astype(float32)
        mask_count = (256.0 * jnp.sum(counts[:, :, 0]) + jnp.sum(counts[:, :, 1])) / block
    else:
        (embed_weight, small_whole, qkv_weight), (out_weight, up_weight), (
            head_weight,
            down_weight,
        ) = [
            [lax.all_gather(shard, "fsdp", axis=0, tiled=True) for shard in shards]
            for shards in groups_low
        ]
        mask_count = wires.total(jnp.full((8, 128), mask_local))[0, 0]
    params_small = jnp.concatenate(
        [small_whole[:, :used], small_whole[:, half : half + SMALL_ROWS - used]], axis=1
    ).T.astype(float32)

    down_moment, down_master = muon_down.T, w_down.T
    stride = -(-D // dp_size // 128) * 128
    share = max(FF // dp_size, 3 * stride)
    def sub_columns(parts):
        return side_by_side([dp_columns(wires, item) for item in parts], stride, share)

    def thirds(values):
        return [values[:, index * D : (index + 1) * D] for index in range(3)]

    moment_parts = jnp.stack(
        [
            padded_to(dp_columns(wires, down_moment), share),
            sub_columns(thirds(muon_qkv)),
            sub_columns([muon_square[index] for index in range(3)]),
            padded_to(dp_columns(wires, muon_up), share),
        ]
    )
    if staged:
        moment_parts = after(moment_parts, embed_weight)

    def send_groups(blocks):
        mine = wires.group
        got = [lax.dynamic_index_in_dim(blocks, mine, 0, keepdims=False)]
        for step in (1, 2, 3):
            sent = lax.dynamic_index_in_dim(blocks, mine ^ step, 0, keepdims=False)
            got.append(wires.swap_mask(sent, step << wires.near_bit))
        return got

    def by_group(got):
        got = jnp.stack(got)
        return jnp.stack(
            [
                lax.dynamic_index_in_dim(got, group ^ wires.group, 0, keepdims=False)
                for group in range(4)
            ]
        )

    def across_groups(blocks):
        return by_group(send_groups(blocks))

    moments_got = send_groups(moment_parts)

    long_table, short_table = interp_tables()
    table = jnp.where(long_image, long_table, short_table)
    position = params_small[14 + UP_ROWS : SMALL_ROWS]
    pixels = jnp.pad(patches[0], ((0, TOKENS - PATCHES), (0, 0)))
    is_patch = (row < PATCHES)[:, None]
    is_class = (row == CLASS_ROW)[:, None]
    embedded = jnp.where(
        chosen[:, None], params_small[1], dot_nn(pixels, embed_weight) + params_small[0]
    )
    embedded = jnp.where(is_patch, embedded, jnp.where(is_class, params_small[2], 0.0))
    resid_first = embedded + jnp.dot(table, position, precision=lax.Precision.HIGHEST)
    if staged:
        middle_own = doubled(wires, middle_own, near_bit, (resid_first,))
        middle = Streams(wires, in_order(wires, middle_own), half_widths[1], 512)
        late_own = after(late_own, middle.first, middle.last)
    unit_first, inverse_first = normalized(resid_first)
    normed_first = (unit_first * params_small[3] + params_small[4]).astype(bfloat)
    qkv_bias = jnp.concatenate([params_small[12], jnp.zeros((D,), float32), params_small[13]])
    mixed = (dot_nn(normed_first, qkv_weight) + qkv_bias).astype(bfloat)
    pixels_both = (pixels, wires.swap(pixels, wires.core_bit))
    mixed, *pixels_both = together(mixed, *pixels_both)
    first_both = (normed_first, wires.swap(normed_first, wires.core_bit))
    keep = ((row < patch_limit) | (row == CLASS_ROW)).astype(float32)[:, None]
    if staged:
        late_own = doubled(wires, late_own, far_bit, (mixed,))
        middle.near((mixed,))
        mixed = after(mixed, middle.first, middle.last, late_own)
        middle.send_far()
    context_low, logsum = attend_forward(mixed, keep)
    context_low, *first_both = together(context_low, *first_both)
    if staged:
        late_own = doubled(wires, late_own, near_bit, (context_low,))
        late = Streams(wires, in_order(wires, late_own), half_widths[2], 512)
        middle.far((context_low, late.first))
        out_weight, up_weight = middle.finish()
    context_both = (context_low, wires.swap(context_low, wires.core_bit))
    resid_second = resid_first + dot_nn(context_low, out_weight) + params_small[5]
    unit_second, inverse_second = normalized(resid_second)
    normed_second = (unit_second * params_small[6] + params_small[7]).astype(bfloat)
    up_bias = params_small[14 : 14 + UP_ROWS].reshape(-1)
    if staged:
        late.near((normed_second,))
        normed_second = after(normed_second, late.first, late.last)
        late.send_far()
    second_both = (normed_second, wires.swap(normed_second, wires.core_bit))
    activ_low, slope = up_forward(normed_second, up_weight, up_bias[None])
    activ_low, moments_got[1], context_other, second_other = together(
        activ_low, moments_got[1], context_both[1], second_both[1]
    )
    context_both, second_both = (context_low, context_other), (normed_second, second_other)
    if staged:
        late.far((activ_low,))
        head_weight, down_weight = late.finish()
    activ_both = (activ_low[None], wires.swap(activ_low, wires.core_bit)[None])
    resid_third = resid_second + dot_nt(activ_low, down_weight) + params_small[8]
    unit_final, inverse_final = normalized(resid_third)
    normed_final = (unit_final * params_small[9] + params_small[10]).astype(bfloat)
    predicted = dot_nn(normed_final, head_weight) + params_small[11]
    residual_error = predicted - pixels.astype(float32)
    loss_local = jnp.sum(chosen_float * residual_error * residual_error)

    core = wires.core_bit
    select = own_selection(wires)

    def other(values):
        return wires.swap(values, core)

    x_order = wires.dp_bits + wires.row_bits
    y_order = wires.row_bits + wires.dp_bits

    def both(values):
        return values, other(values)

    def both(values):
        return values, other(values)

    part_width = D // dp_size

    def blocks(values):
        return values.reshape(4, block, values.shape[-1])

    def wide_part(flows):
        return jnp.concatenate([blocks(item.plain[0]) for item in flows], axis=-1)

    def extra_part(flows):
        return blocks(next(item.plain[1] for item in flows if len(item.plain) > 1))

    near, far = wires.bit(wires.near_bit), wires.bit(wires.far_bit)

    def pick(flag, first, second):
        return jnp.where(flag == 0, first, second)

    class near_stage:
        def __init__(self, first, second, exact=None):
            self.keep, self.exact = pick(near, first, second), None
            parts = [pick(near, second, first).astype(bfloat)]
            if exact is not None:
                self.exact = pick(near, *exact)
                parts.append(split_exact(pick(near, exact[1], exact[0])))
            self.sent = jnp.concatenate(parts, axis=-1)
            self.got = wires.swap(self.sent, wires.near_bit)

        def land(self, hold=()):
            got = after(self.got, *hold) if hold else self.got
            width = self.keep.shape[-1]
            total = self.keep + got[..., :width].astype(float32)
            if self.exact is None:
                return total, None
            return total, self.exact + joined_exact(got[..., width:])

    def flow(pairs, order, exact=None):
        return Flow(wires, None).first(
            [(fold(near), fold(away)) for near, away in pairs], order[0], exact
        )

    def onward(flows, orders, hold=()):
        for item, order in zip(flows, orders):
            for bit in order[1:]:
                item.next(bit, hold)
        return [item.sent[-1] for item in flows]

    grad_pred = 2.0 / mask_count * chosen_float * residual_error
    pred_low = grad_pred.astype(bfloat)
    head_pair = pair_grad(wires, select, both(normed_final), both(pred_low[None]), False)
    grad_head_bias = jnp.sum(grad_pred, axis=0, keepdims=True)
    grad_normed = dot_nt(pred_low, head_weight)
    grad_resid, gain_final, shift_final = norm_backward(
        grad_normed, unit_final, inverse_final, params_small[9]
    )
    branch_low = grad_resid.astype(bfloat)
    branch_both = both(branch_low)
    down_pairs = [
        pair_grad(wires, select, branch_both, activ_both, cut == 1, cut=cut) for cut in range(2)
    ]
    down_flows = [flow([down_pairs[0], head_pair], x_order), flow(down_pairs[1:], y_order)]
    grad_down_bias = jnp.sum(grad_resid, axis=0, keepdims=True)
    hidden_low, grad_up_bias = hidden_backward(
        after(branch_low, *(item.sent[0] for item in down_flows)), down_weight, slope
    )
    hidden_both = both(hidden_low[None])
    grad_normed = dot_nt(hidden_low, up_weight)
    grad_part, gain_second, shift_second = norm_backward(
        grad_normed, unit_second, inverse_second, params_small[6]
    )
    grad_resid = grad_resid + grad_part
    branch_low = grad_resid.astype(bfloat)
    normed_both = second_both
    up_first = pair_grad(
        wires, select, normed_both, (after(hidden_both[0], branch_low), hidden_both[1]), False, cut=0
    )
    up_last = pair_grad(
        wires, select, normed_both, (after(hidden_both[0], up_first[1]), hidden_both[1]), True, cut=1
    )
    out_pair = pair_grad(
        wires, select, context_both, (after(branch_low, up_last[1])[None], other(branch_low)[None]),
        True,
    )
    up_flows = [flow([up_first], x_order), flow([up_last, out_pair], y_order)]
    grad_out_bias = jnp.sum(grad_resid, axis=0, keepdims=True)
    grad_context = dot_nt(after(branch_low, out_pair[1]), out_weight).astype(bfloat)
    sent = onward(down_flows, [x_order, y_order], (grad_context,))
    grad_context = after(grad_context, *sent, *(item.sent[-1] for item in up_flows))
    normed_both = first_both
    if dp_size == 2:
        away_low, away_sums = attend_backward(mixed, grad_context, logsum, keep, 1 - wires.dp, 2)
        away_both = both(away_low)
        for item in down_flows:
            item.land((away_low,))
        sent = onward(up_flows, [x_order, y_order], (away_low, *(item.plain[0] for item in down_flows)))
        away_pair = pair_product(
            select, normed_both, (after(away_both[0], *sent), away_both[1]), bfloat
        )
        grad_context = after(grad_context, away_pair)
        near_low, near_sums = attend_backward(mixed, grad_context, logsum, keep, wires.dp, 2)
        near_both = both(near_low)
        near_pair = pair_product(select, normed_both, near_both, float32)
        qkv_flow = Flow(wires, None).first([(near_pair[None], away_pair[None])], x_order[0])
        grad_normed = mixed_backward(wires.dp, away_low, after(near_low, near_pair), qkv_weight)
        for item in up_flows:
            item.land((grad_normed,))
        wide_near = near_stage(wide_part(down_flows), wide_part(up_flows))
        grad_normed = after(grad_normed, wide_near.sent)
        bias_sums = jnp.where(
            wires.dp == 0,
            jnp.concatenate([near_sums, away_sums], axis=1),
            jnp.concatenate([away_sums, near_sums], axis=1),
        )
    else:
        mixed_low, bias_sums = attend_backward(
            mixed, grad_context, logsum, keep, jnp.zeros((), jnp.int32), 1
        )
        for item in down_flows:
            item.land((mixed_low,))
        sent = onward(up_flows, [x_order, y_order], (mixed_low,))
        qkv_pair = pair_grad(wires, select, normed_both, both(mixed_low), False)
        qkv_flow = flow([qkv_pair], x_order)
        for item in up_flows:
            item.land()
        wide_near = near_stage(wide_part(down_flows), wide_part(up_flows))
        grad_normed = sum(dot_nt(mixed_low[i], thirds(qkv_weight)[i]) for i in range(3))
    grad_part, gain_first, shift_first = norm_backward(
        grad_normed, unit_first, inverse_first, params_small[3]
    )
    grad_resid = grad_resid + grad_part
    unchosen = jnp.where(is_patch & ~chosen[:, None], grad_resid, 0.0)
    unchosen_low = unchosen.astype(bfloat)
    unchosen_both = both(unchosen_low[None])
    sent = onward([qkv_flow], [x_order], (unchosen_low,))
    grad_resid = after(grad_resid, *sent)
    grad_leading = grad_resid[CLASS_ROW : CLASS_ROW + 1]
    grad_position = lax.dot_general(
        table, grad_resid, (((0,), (0,)), ((), ())), precision=lax.Precision.HIGHEST
    )
    grad_mask_token = jnp.sum(jnp.where(chosen[:, None], grad_resid, 0.0), axis=0, keepdims=True)
    grad_patch_bias = jnp.sum(unchosen, axis=0, keepdims=True)
    small_parts = [
        grad_patch_bias,
        grad_mask_token,
        grad_leading,
        gain_first,
        shift_first,
        grad_out_bias,
        gain_second,
        shift_second,
        grad_down_bias,
        gain_final,
        shift_final,
        grad_head_bias,
        bias_sums,
        grad_up_bias.reshape(UP_ROWS, D),
        grad_position,
    ]
    small_parts[-1] = after(grad_position, unchosen_both[1])
    grad_small = stacked_rows(small_parts, SMALL_PAD)

    wide_half, unused = wide_near.land((grad_small,))
    wide_far = wide_half.astype(bfloat)
    far_mask = 1 << wires.far_bit
    places = [((i >> wires.near_bit) & 1, (i >> wires.far_bit) & 1, i) for i in range(wires.count)]
    wide_got = lax.ppermute(
        wide_far, BOTH, [(i, i ^ far_mask) for n, f, i in places if n != f]
    )
    unchosen_both = (after(unchosen_both[0], wide_far), unchosen_both[1])
    patch_pair = pair_grad(wires, select, pixels_both, unchosen_both, False)

    tail = half // dp_size
    grad_small = grad_small + other(grad_small)
    grad_small = grad_small.reshape(2, dp_size, tail, D)
    grad_small = jnp.stack(
        [
            lax.dynamic_index_in_dim(grad_small, wires.dp ^ distance, 1, keepdims=False)
            for distance in range(dp_size)
        ]
    ).reshape(SMALL_PAD, D)
    layers, rest = [], grad_small
    for layer in range(3):
        layers.append(rest.astype(bfloat))
        rest = rest - layers[-1].astype(float32)
    small_own = sum(dot_nt(select, layer) for layer in layers)
    small_own = small_own.reshape(D // 2, dp_size, 2 * tail).transpose(1, 0, 2)
    patch_flow = flow([patch_pair], x_order, small_own)
    qkv_flow.land((patch_flow.sent[0],))
    onward([patch_flow], [x_order], (moments_got[2], *qkv_flow.plain))
    patch_flow.land((moments_got[3],))

    qkv_part = blocks(qkv_flow.plain[0])
    square_part = jnp.concatenate(
        [blocks(patch_flow.plain[0]), extra_part(up_flows), extra_part(down_flows)], axis=-1
    )
    small_part = blocks(patch_flow.exact)
    small_low_part, small_high_part = small_part[..., :tail], small_part[..., tail:]
    wide_sum = wide_half + after(wide_got, *patch_flow.sent).astype(float32)
    narrow_sum, small_sum = near_stage(
        after(square_part, wide_sum), qkv_part, (small_low_part, small_high_part)
    ).land()
    narrow_got = lax.ppermute(
        jnp.concatenate([narrow_sum.astype(bfloat), split_exact(small_sum)], axis=-1),
        BOTH,
        [(i, i ^ far_mask) for n, f, i in places if n == f],
    )
    narrow_sum = narrow_sum + narrow_got[..., : 3 * part_width].astype(float32)
    small_sum = small_sum + joined_exact(narrow_got[..., 3 * part_width :])
    narrow_sum = side_by_side(
        [narrow_sum[..., i * part_width : (i + 1) * part_width] for i in range(3)], stride, share
    )
    outer = near ^ far
    own_grad = pick(outer, padded_to(wide_sum, share), narrow_sum)
    own_small = pick(outer, jnp.zeros_like(small_sum), small_sum)
    own_grad, own_small = lax.optimization_barrier((own_grad, own_small))


    squares_local = jnp.sum(own_grad * own_grad) + jnp.sum(own_small * own_small)
    lane = lax.broadcasted_iota(jnp.int32, (8, 128), 1)
    scalars = wires.total(jnp.where(lane == 0, loss_local, squares_local))
    loss_sum = scalars[0, 0]
    grad_norm = jnp.sqrt(scalars[0, 1])
    factor = jnp.minimum(1.0, clip_limit / (grad_norm + 1e-06))

    own_moment = by_group(moments_got)
    grad_blocks = jnp.concatenate([own_grad.astype(bfloat), split_exact(own_small)], axis=-1)
    grad_blocks = after(grad_blocks, factor)
    grads_got = send_groups(grad_blocks)
    clipped = own_grad * factor
    blend = clipped + momentum_decay * (momentum_decay * own_moment + clipped)
    blend_low = blend.astype(bfloat)
    half_rows = 2 * block
    dps, rows = wires.dp_bits, wires.row_bits
    upper, lower = blend_low[:2].reshape(half_rows, share), blend_low[2:].reshape(half_rows, share)
    orders = list(zip(dps + rows, rows + dps))
    for turn, (upper_bit, lower_bit) in enumerate(orders):
        upper_got, lower_got = wires.swap(upper, upper_bit), wires.swap(lower, lower_bit)
        if turn < 2:
            upper_got, lower_got, grads_got[turn + 1] = together(
                upper_got, lower_got, grads_got[turn + 1]
            )
        upper, lower = jnp.stack([upper, upper_got]), jnp.stack([lower, lower_got])
    own_pieces = jnp.concatenate(
        [upper.reshape(-1, half_rows, share), lower.reshape(-1, half_rows, share)]
    )
    other_pieces = other(own_pieces)
    other_pieces, grads_got[3] = together(other_pieces, grads_got[3])
    grad_rows = by_group(grads_got)
    grad_all = gather_relative(wires, grad_rows, dps).reshape((dp_size,) + grad_rows.shape)
    own_pieces = after(own_pieces, grad_rows)
    squares_flag = (wires.group == 2).astype(jnp.int32).reshape(1)
    ortho = orthogonalize(
        squares_flag, own_pieces, other_pieces, 1 << len(rows), dp_size, stride, 4 * block
    )

    updates_got = send_groups(ortho.reshape(4, block, ortho.shape[1]))

    def joined(parts):
        parts = jnp.stack(parts)
        return jnp.concatenate(
            [
                lax.dynamic_index_in_dim(parts, place ^ wires.dp, 0, keepdims=False)
                for place in range(dp_size)
            ],
            axis=-1,
        ).astype(float32)

    def grad_columns(task, start, width):
        part = width // dp_size
        return joined([grad_all[far, task, :, start : start + part] for far in range(dp_size)])

    def update_columns(task, start, width, spread):
        part = width // dp_size
        return joined(
            [
                updates[task, :, far * spread + start : far * spread + start + part]
                for far in range(dp_size)
            ]
        )

    def three_grads(task):
        return [grad_columns(task, index * stride, D) for index in range(3)]

    grads = [
        jnp.stack(three_grads(2)),
        jnp.concatenate(three_grads(1), axis=1),
        grad_columns(3, 0, FF),
        grad_columns(0, 0, FF),
    ]
    olds = [muon_square, muon_qkv, muon_up, down_moment]
    masters = [w_square, w_qkv, w_up, down_master]
    new_moments = [
        momentum_decay * old + factor * fresh for old, fresh in zip(olds, grads)
    ]
    small_grad = jnp.concatenate(
        [
            grad_columns(task, share, half) + grad_columns(task, share + tail, half)
            for task in (2, 1)
        ],
        axis=1,
    )[:, :SMALL_ROWS].T
    small_grad = small_grad * factor
    new_first = beta_first * adam_first + (1.0 - beta_first) * small_grad
    new_second = beta_second * adam_second + (1.0 - beta_second) * small_grad * small_grad
    first_hat = new_first / (1.0 - beta_first**STEP)
    second_hat = new_second / (1.0 - beta_second**STEP)
    new_small = small - adam_rate * first_hat / (jnp.sqrt(second_hat) + adam_eps)
    early_outs = (*new_moments, new_small, new_first, new_second)
    updates_got, early_outs = lax.optimization_barrier((updates_got, early_outs))
    *new_moments, new_small, new_first, new_second = early_outs
    updates = by_group(updates_got)
    ups = [
        jnp.stack([update_columns(2, index * dp_size * stride, D, stride) for index in range(3)]),
        jnp.concatenate(
            [update_columns(1, index * stride, D, share) for index in range(3)], axis=1
        ),
        update_columns(3, 0, FF, share),
        update_columns(0, 0, FF, share),
    ]
    new_weights = [
        master * (1.0 - muon_rate * muon_decay)
        - muon_rate * 0.2 * math.sqrt(master.shape[-1]) * update
        for master, update in zip(masters, ups)
    ]
    return (
        loss_sum,
        mask_count,
        grad_norm,
        new_weights[0],
        new_moments[0],
        new_weights[1],
        new_moments[1],
        new_weights[2],
        new_moments[2],
        new_weights[3].T,
        new_moments[3].T,
        new_small,
        new_first,
        new_second,
    )


def solution(mesh):
    placed = (
        P(("fsdp", "dp"), None, None),
        P(("fsdp", "dp"), None),
        P(("fsdp", "dp")),
        P(None, "fsdp", None),
        P("fsdp", None),
        P("fsdp", None),
        P(None, "fsdp"),
        P(None, "fsdp"),
        P(None, "fsdp", None),
        P("fsdp", None),
        P("fsdp", None),
        P(None, "fsdp"),
        P(None, "fsdp"),
        P(None, "fsdp"),
    )
    return jax.shard_map(
        per_device,
        mesh=mesh,
        in_specs=placed,
        out_specs=(
            P(),
            P(),
            P(),
            P(None, "fsdp", None),
            P(None, "fsdp", None),
            P("fsdp", None),
            P("fsdp", None),
            P("fsdp", None),
            P("fsdp", None),
            P(None, "fsdp"),
            P(None, "fsdp"),
            P(None, "fsdp"),
            P(None, "fsdp"),
            P(None, "fsdp"),
        ),
        check_vma=False,
    )
```

```python
from functools import partial
import math

import jax
import jax.numpy as jnp
import numpy as np
from jax import lax
from jax.experimental import pallas as pl
from jax.experimental.pallas import tpu as pltpu
from jax.sharding import PartitionSpec as P

D = 768
FF = 3072
HEADS = 12
HEAD_DIM = 64
GRID = 24
SHORT_GRID = 14
NS_ITERS = 5
STEP = 10
PATCHES = 576
SHORT_PATCHES = 196
UP_ROWS = FF // D
POS = SHORT_PATCHES + 1
SMALL_ROWS = 14 + UP_ROWS + POS
CLASS_ROW = PATCHES
TOKENS = 592
SMALL_PAD = 256
MIB = 1024 * 1024
SCALE = HEAD_DIM**-0.5

layer_eps = 1e-06
coeff_first, coeff_second, coeff_third = (3.4445, -4.775, 2.0315)
momentum_decay = 0.95
muon_rate = 0.15
muon_decay = 0.01
beta_first = 0.9
beta_second = 0.999
adam_rate = 0.3
adam_eps = 1e-08
clip_limit = 0.5
masked_score = -1000000000.0

BOTH = ("fsdp", "dp")
bfloat = jnp.bfloat16
float32 = jnp.float32


def interp_tables():
    axis_table = np.zeros((GRID, SHORT_GRID), np.float64)
    for target in range(GRID):
        source = (target + 0.5) * SHORT_GRID / GRID - 0.5
        source = min(max(source, 0.0), SHORT_GRID - 1.0)
        below = int(math.floor(source))
        above = min(below + 1, SHORT_GRID - 1)
        axis_table[target, below] += 1.0 - (source - below)
        axis_table[target, above] += source - below
    axis_table = axis_table.astype(np.float32)
    long_table = np.zeros((TOKENS, POS), np.float32)
    long_table[:PATCHES, 1:] = np.kron(axis_table, axis_table)
    long_table[CLASS_ROW, 0] = 1.0
    short_table = np.zeros((TOKENS, POS), np.float32)
    short_table[:SHORT_PATCHES, 1:] = np.eye(SHORT_PATCHES)
    short_table[CLASS_ROW, 0] = 1.0
    return long_table, short_table


def cost(flops, bytes_accessed, transcendentals):
    return pl.CostEstimate(
        flops=flops, bytes_accessed=bytes_accessed, transcendentals=0
    )


def dot_nt(left, right):
    return lax.dot_general(left, right, (((1,), (1,)), ((), ())), preferred_element_type=float32)


def dot_nn(left, right):
    return lax.dot_general(left, right, (((1,), (0,)), ((), ())), preferred_element_type=float32)


def dot_tn(left, right):
    return lax.dot_general(left, right, (((0,), (0,)), ((), ())), preferred_element_type=float32)


def attend_forward_kernel(q_ref, k_ref, v_ref, keep_ref, context_ref, logsum_ref):
    keep = keep_ref[...] > 0
    outs = []
    for head in range(2):
        cols = slice(HEAD_DIM * head, HEAD_DIM * (head + 1))
        query, key, value = q_ref[:, cols] * SCALE, k_ref[:, cols], v_ref[:, cols]
        scores = jnp.where(keep, dot_nt(key, query), masked_score)
        peak = jnp.max(scores, axis=0, keepdims=True)
        expo = jnp.exp(scores - peak)
        total = jnp.sum(expo, axis=0, keepdims=True)
        probs = (expo * (1.0 / total)).astype(bfloat)
        outs.append(dot_nn(value.T, probs).T.astype(bfloat))
        logsum_ref[head] = peak + jnp.log(total)
    context_ref[...] = jnp.concatenate(outs, axis=1)


def attend_backward_kernel(
    place_ref, q_ref, k_ref, v_ref, grad_ref, logsum_ref, keep_ref, mixed_ref, sums_ref
):
    keep = keep_ref[...] > 0
    grads_query, grads_key, grads_value = [], [], []
    for head in range(2):
        cols = slice(HEAD_DIM * head, HEAD_DIM * (head + 1))
        query, key, value, grad = q_ref[:, cols], k_ref[:, cols], v_ref[:, cols], grad_ref[:, cols]
        query, scaled_key = query * SCALE, key * SCALE
        scores = dot_nt(key, query)
        probs = jnp.where(keep, jnp.exp(scores - logsum_ref[head]), 0.0)
        grad_probs = dot_nt(value, grad)
        grads_value.append(dot_nn(probs.astype(bfloat), grad))
        mixed = probs * grad_probs
        total = jnp.sum(mixed, axis=0, keepdims=True)
        scores_low = (mixed - probs * total).astype(bfloat)
        grads_key.append(dot_nn(scores_low, query))
        grads_query.append(dot_nn(scaled_key.T, scores_low).T)
    grad_query = jnp.concatenate(grads_query, axis=1)
    grad_value = jnp.concatenate(grads_value, axis=1)
    mixed_ref[0] = grad_query.astype(bfloat)
    mixed_ref[1] = jnp.concatenate(grads_key, axis=1).astype(bfloat)
    mixed_ref[2] = grad_value.astype(bfloat)
    sums_ref[0:1, :] = jnp.sum(grad_query, axis=0, keepdims=True)
    sums_ref[1:2, :] = jnp.sum(grad_value, axis=0, keepdims=True)


def head_block(offset):
    return pl.BlockSpec((TOKENS, 2 * HEAD_DIM), lambda pair: (0, offset + pair))


KEEP_BLOCK = pl.BlockSpec((TOKENS, 1), lambda pair: (0, 0))
LOGSUM_BLOCK = pl.BlockSpec((2, 1, TOKENS), lambda pair: (pair, 0, 0))
PAIRS = HEADS // 2


def attend_forward(mixed, keep):
    return pl.pallas_call(
        attend_forward_kernel,
        grid=(PAIRS,),
        in_specs=[head_block(0), head_block(PAIRS), head_block(2 * PAIRS), KEEP_BLOCK],
        out_specs=[head_block(0), LOGSUM_BLOCK],
        out_shape=[
            jax.ShapeDtypeStruct((TOKENS, D), bfloat),
            jax.ShapeDtypeStruct((HEADS, 1, TOKENS), float32),
        ],
        cost_estimate=cost(
            flops=8 * TOKENS * TOKENS * D, bytes_accessed=8 * TOKENS * D, transcendentals=0
        ),
        compiler_params=pltpu.CompilerParams(vmem_limit_bytes=18 * MIB),
    )(mixed, mixed, mixed, keep)


def attend_backward(mixed, grad, logsum, keep, part, count):
    pairs = PAIRS // count
    lanes = 2 * HEAD_DIM

    def block(offset):
        return pl.BlockSpec((TOKENS, lanes), lambda pair, place: (0, offset + place[0] * pairs + pair))

    return pl.pallas_call(
        attend_backward_kernel,
        grid_spec=pltpu.PrefetchScalarGridSpec(
            num_scalar_prefetch=1,
            grid=(pairs,),
            in_specs=[
                block(0),
                block(PAIRS),
                block(2 * PAIRS),
                block(0),
                pl.BlockSpec((2, 1, TOKENS), lambda pair, place: (place[0] * pairs + pair, 0, 0)),
                pl.BlockSpec((TOKENS, 1), lambda pair, place: (0, 0)),
            ],
            out_specs=[
                pl.BlockSpec((3, TOKENS, lanes), lambda pair, place: (0, 0, pair)),
                pl.BlockSpec((2, lanes), lambda pair, place: (0, pair)),
            ],
        ),
        out_shape=[
            jax.ShapeDtypeStruct((3, TOKENS, pairs * lanes), bfloat),
            jax.ShapeDtypeStruct((2, pairs * lanes), float32),
        ],
        cost_estimate=cost(
            flops=20 * TOKENS * TOKENS * pairs * lanes,
            bytes_accessed=16 * TOKENS * pairs * lanes,
            transcendentals=0,
        ),
        compiler_params=pltpu.CompilerParams(vmem_limit_bytes=20 * MIB),
    )(part.reshape(1).astype(jnp.int32), mixed, mixed, mixed, grad, logsum, keep)


def stack_kernel(*refs):
    out_ref, start = refs[-1], 0
    for ref in refs[:-1]:
        out_ref[start : start + ref.shape[0], :] = ref[...]
        start += ref.shape[0]
    out_ref[start:, :] = jnp.zeros((out_ref.shape[0] - start, out_ref.shape[1]), out_ref.dtype)


def stacked_rows(parts, count):
    return pl.pallas_call(
        stack_kernel, out_shape=jax.ShapeDtypeStruct((count, parts[0].shape[1]), float32)
    )(*parts)


def gelu_parts(values):
    size = 1.0 + 0.23164189 * jnp.abs(values)
    inner = 1.0 / size
    poly = jnp.full_like(inner, 0.5 * 1.061405429)
    for coeff in (-1.453152027, 1.421413741, -0.284496736, 0.254829592):
        poly = poly * inner + 0.5 * coeff
    bell = jnp.exp(-0.5 * values * values)
    tail = poly * inner * bell
    below = jnp.where(values >= 0.0, 1.0 - tail, tail)
    return values * below, below + values * (0.3989422804014327 * bell)


UP_TILE = 768
UP_ROW_TILE = 160


def up_kernel(normed_ref, weight_ref, bias_ref, activ_ref, slope_ref):
    for start in range(0, TOKENS, UP_ROW_TILE):
        rows = slice(start, min(start + UP_ROW_TILE, TOKENS))
        hidden = dot_nn(normed_ref[rows], weight_ref[...]) + bias_ref[...]
        activ, slope = gelu_parts(hidden)
        activ_ref[rows] = activ.astype(bfloat)
        slope_ref[rows] = slope


def up_forward(normed, weight, bias):
    tile = pl.BlockSpec((TOKENS, UP_TILE), lambda step: (0, step))
    return pl.pallas_call(
        up_kernel,
        grid=(FF // UP_TILE,),
        in_specs=[
            pl.BlockSpec((TOKENS, D), lambda step: (0, 0)),
            pl.BlockSpec((D, UP_TILE), lambda step: (0, step)),
            pl.BlockSpec((1, UP_TILE), lambda step: (0, step)),
        ],
        out_specs=[tile, tile],
        out_shape=[
            jax.ShapeDtypeStruct((TOKENS, FF), bfloat),
            jax.ShapeDtypeStruct((TOKENS, FF), float32),
        ],
        cost_estimate=cost(
            flops=2 * TOKENS * D * FF, bytes_accessed=20 * MIB, transcendentals=0
        ),
        compiler_params=pltpu.CompilerParams(vmem_limit_bytes=20 * MIB),
    )(normed, weight, bias)


def hidden_kernel(branch_ref, weight_ref, slope_ref, hidden_ref, sums_ref):
    grad = dot_nn(branch_ref[...], weight_ref[...]) * slope_ref[...]
    hidden_ref[...] = grad.astype(bfloat)
    sums_ref[...] = jnp.sum(grad, axis=0, keepdims=True)


def hidden_backward(branch, weight, slope):
    tile = pl.BlockSpec((TOKENS, UP_TILE), lambda step: (0, step))
    return pl.pallas_call(
        hidden_kernel,
        grid=(FF // UP_TILE,),
        in_specs=[
            pl.BlockSpec((TOKENS, D), lambda step: (0, 0)),
            pl.BlockSpec((D, UP_TILE), lambda step: (0, step)),
            tile,
        ],
        out_specs=[tile, pl.BlockSpec((1, UP_TILE), lambda step: (0, step))],
        out_shape=[
            jax.ShapeDtypeStruct((TOKENS, FF), bfloat),
            jax.ShapeDtypeStruct((1, FF), float32),
        ],
        cost_estimate=cost(
            flops=2 * TOKENS * D * FF, bytes_accessed=20 * MIB, transcendentals=0
        ),
        compiler_params=pltpu.CompilerParams(vmem_limit_bytes=20 * MIB),
    )(branch, weight, slope)


def normalized(values):
    centred = values - jnp.mean(values, axis=-1, keepdims=True)
    variance = jnp.mean(centred * centred, axis=-1, keepdims=True)
    inverse = lax.rsqrt(variance + layer_eps)
    return centred * inverse, inverse


def norm_backward(grad, unit, inverse, gain):
    grad_unit = grad * gain
    mean_grad = jnp.mean(grad_unit, axis=-1, keepdims=True)
    mean_mixed = jnp.mean(grad_unit * unit, axis=-1, keepdims=True)
    grad_values = inverse * (grad_unit - mean_grad - unit * mean_mixed)
    return (
        grad_values,
        jnp.sum(grad * unit, axis=0, keepdims=True),
        jnp.sum(grad, axis=0, keepdims=True),
    )


TILE = 256


def ortho_kernel(squares_ref, own_ref, other_ref, out_ref, full_ref, gram_ref, poly_ref, *, places, shares, stride):
    rows, share = own_ref.shape[1], own_ref.shape[2]
    own_rows = out_ref.shape[0]
    width = shares * stride

    def pieces():
        for core, ref in enumerate((own_ref, other_ref)):
            for place in range(places):
                for part in range(2):
                    for column in range(shares):
                        index = place * shares + column if part == 0 else column * places + place
                        top = core * (D // 2) + (2 * place + part) * rows
                        yield ref, part * places * shares + index, top, column

    def inverse_norm(total):
        return 1.0 / (jnp.sqrt(total) + 1e-07)

    def mirrored(ref, make):
        for i in range(D // TILE):
            ref[i * TILE : (i + 1) * TILE, : (i + 1) * TILE] = make(i).astype(bfloat)
            for j in range(i):
                block = ref[i * TILE : (i + 1) * TILE, j * TILE : (j + 1) * TILE]
                ref[j * TILE : (j + 1) * TILE, i * TILE : (i + 1) * TILE] = block.T

    def grams(start, columns):
        def gram(i):
            return dot_nt(
                full_ref[i * TILE : (i + 1) * TILE, pl.ds(start, columns)],
                full_ref[: (i + 1) * TILE, pl.ds(start, columns)],
            )

        def poly(i):
            block = gram_ref[i * TILE : (i + 1) * TILE, :]
            product = dot_nn(block, gram_ref[:, : (i + 1) * TILE])
            return coeff_second * block[:, : (i + 1) * TILE].astype(float32) + coeff_third * product

        mirrored(gram_ref, gram)
        mirrored(poly_ref, poly)

    def step(start, columns, tall, target):
        old = full_ref[:, pl.ds(start, columns)]
        fresh = coeff_first * old[:tall].astype(float32) + dot_nn(poly_ref[:tall, :], old)
        target[:tall, pl.ds(start, columns)] = fresh.astype(bfloat)

    @pl.when(squares_ref[0] == 0)
    def one_matrix():
        total = jnp.zeros((), float32)
        for ref in (own_ref, other_ref):
            for index in range(ref.shape[0]):
                values = ref[index].astype(float32)
                total = total + jnp.sum(values * values)
        scale = inverse_norm(total)
        for ref, index, top, column in pieces():
            full_ref[top : top + rows, column * share : (column + 1) * share] = (
                ref[index].astype(float32) * scale
            ).astype(bfloat)
        columns = shares * share

        @pl.loop(0, NS_ITERS - 1)
        def sweep(index):
            grams(0, columns)
            step(0, columns, D, full_ref)

        grams(0, columns)
        step(0, columns, own_rows, out_ref)

    @pl.when(squares_ref[0] != 0)
    def three_matrices():
        for square in range(3):
            part = slice(square * stride, (square + 1) * stride)
            total = jnp.zeros((), float32)
            for ref in (own_ref, other_ref):
                for index in range(ref.shape[0]):
                    values = ref[index, :, part].astype(float32)
                    total = total + jnp.sum(values * values)
            scale = inverse_norm(total)
            for ref, index, top, column in pieces():
                left = square * width + column * stride
                full_ref[top : top + rows, left : left + stride] = (
                    ref[index, :, part].astype(float32) * scale
                ).astype(bfloat)

        @pl.loop(0, 3)
        def one(square):
            start = pl.multiple_of(square * width, 128)

            @pl.loop(0, NS_ITERS - 1)
            def sweep(index):
                grams(start, width)
                step(start, width, D, full_ref)

            grams(start, width)
            step(start, width, own_rows, out_ref)


def orthogonalize(squares, own, other, places, shares, stride, own_rows):
    count, rows, share = own.shape
    columns = max(shares * share, 3 * shares * stride)
    return pl.pallas_call(
        partial(ortho_kernel, places=places, shares=shares, stride=stride),
        in_specs=[
            pl.BlockSpec(memory_space=pltpu.SMEM),
            pl.BlockSpec(memory_space=pltpu.VMEM),
            pl.BlockSpec(memory_space=pltpu.VMEM),
        ],
        out_specs=pl.BlockSpec(memory_space=pltpu.VMEM),
        out_shape=jax.ShapeDtypeStruct((own_rows, columns), bfloat),
        scratch_shapes=[
            pltpu.VMEM((D, columns), bfloat),
            pltpu.VMEM((D, D), bfloat),
            pltpu.VMEM((D, D), bfloat),
        ],
        cost_estimate=cost(
            flops=10 * D * D * (2 * FF + D), bytes_accessed=8 * MIB, transcendentals=0
        ),
        compiler_params=pltpu.CompilerParams(vmem_limit_bytes=36 * MIB),
    )(squares, own, other)


class Wires:
    def __init__(self):
        self.fsdp_size, self.dp_size = lax.axis_size("fsdp"), lax.axis_size("dp")
        self.count = self.fsdp_size * self.dp_size
        self.fsdp, self.dp = lax.axis_index("fsdp"), lax.axis_index("dp")
        self.me = self.fsdp * self.dp_size + self.dp
        dp_bits = self.dp_size.bit_length() - 1
        all_bits = self.count.bit_length() - 1
        assert self.count == 1 << all_bits and self.fsdp_size >= 8
        self.dp_bits = list(range(dp_bits))
        self.core_bit = dp_bits
        self.row_bits = list(range(dp_bits + 1, all_bits - 2))
        self.near_bit, self.far_bit = all_bits - 2, all_bits - 1
        self.all_bits = list(range(all_bits))
        self.group = self.me >> self.near_bit

    def bit(self, bit):
        return (self.me >> bit) & 1

    def swap(self, values, bit):
        return self.swap_mask(values, 1 << bit)

    def swap_mask(self, values, mask):
        return lax.ppermute(values, BOTH, [(i, i ^ mask) for i in range(self.count)])

    def total(self, values):
        for bit in [self.core_bit] + self.dp_bits + self.row_bits + [self.near_bit, self.far_bit]:
            values = values + self.swap(values, bit)
        return values


def after(values, *others):
    return lax.optimization_barrier((values,) + others)[0]


def together(*values):
    return lax.optimization_barrier(values)


def split_exact(values):
    high = values.astype(bfloat)
    return jnp.concatenate([high, (values - high.astype(float32)).astype(bfloat)], axis=-1)


def joined_exact(sent):
    width = sent.shape[-1] // 2
    return sent[..., :width].astype(float32) + sent[..., width:].astype(float32)


def own_selection(wires):
    low = wires.fsdp_size // 4
    block = D // wires.fsdp_size
    place = jnp.arange(D // 2)
    distance, group, inner = place // (4 * block), place // block % 4, place % block
    count = len(wires.row_bits)
    flips = sum(
        ((distance >> (count - 1 - i)) & 1) << (bit - wires.core_bit)
        for i, bit in enumerate(wires.row_bits)
    )
    source = (group * low + ((wires.fsdp % low) ^ flips)) * block + inner
    return (source[:, None] == jnp.arange(D)[None, :]).astype(bfloat)


def pair_kernel(
    place_ref, select_ref, left_ref, left_other_ref, right_ref, right_other_ref,
    near_ref, away_ref, rows_ref, rows_other_ref, *, by_rows, halves
):
    @pl.when((pl.program_id(0) == 0) & (pl.program_id(1) == 0) & (pl.program_id(2) == 0))
    def select():
        rows_ref[...] = dot_nt(select_ref[...], left_ref[...]).astype(bfloat)
        rows_other_ref[...] = dot_nt(select_ref[...], left_other_ref[...]).astype(bfloat)

    right = right_ref[...].reshape(right_ref.shape[-2:])
    right_other = right_other_ref[...].reshape(right.shape)
    product = dot_nn(rows_ref[...], right) + dot_nn(rows_other_ref[...], right_other)
    if by_rows:
        half = product.shape[0] // 2
        near_ref[0, 0] = product[:half]
        away_ref[0, 0] = product[half:].astype(bfloat)
    else:

        @pl.when(pl.program_id(0) < halves)
        def away():
            away_ref[0, 0] = product.astype(bfloat)

        @pl.when(pl.program_id(0) >= halves)
        def near():
            near_ref[0, 0] = product


def column_tiles(width, cuts):
    sizes = [size for size in (768, 512, 384, 256, 128) if width % size == 0 and width // size >= cuts]
    return sizes[0] if sizes else width


def pair_grad(wires, select, left, right, by_rows, parts=None, cut=None):
    left, left_other = left
    right, right_other = right
    tokens, columns = right.shape[1:]
    first_part, parts = (0, right.shape[0]) if parts is None else parts
    dp_size = wires.dp_size
    width = columns // dp_size
    halves = dp_size // 2
    tile = column_tiles(width, 1 if cut is None else 2)
    all_steps = width // tile
    first_step, steps = 0, all_steps
    if cut is not None:
        edge = all_steps // 2
        first_step, steps = (0, edge) if cut == 0 else (edge, all_steps - edge)
    if tile % 128:
        right, right_other = (
            item.reshape(item.shape[0], tokens, dp_size, width).transpose(2, 0, 1, 3)
            for item in (right, right_other)
        )

    def distance(turn):
        return turn if by_rows else jnp.where(turn < halves, 2 * turn + 1, 2 * (turn - halves))

    def right_place(turn, part, step, place):
        column = distance(turn) ^ place[0]
        if right.ndim == 4:
            return (column, first_part + part, 0, 0)
        return (first_part + part, 0, column * all_steps + first_step + step)

    right_block = (1, 1, tokens, width) if right.ndim == 4 else (1, tokens, tile)
    rows = D // 2
    if by_rows:
        rows //= 2
        count = dp_size

        def near_place(turn, part, step, place):
            return (turn, part, 0, step)

        away_place = near_place
    else:
        count = halves

        def near_place(turn, part, step, place):
            there = turn >= halves
            return (
                jnp.maximum(turn - halves, 0),
                jnp.where(there, part, 0),
                0,
                jnp.where(there, step, 0),
            )

        def away_place(turn, part, step, place):
            there = turn < halves
            return (
                jnp.minimum(turn, halves - 1),
                jnp.where(there, part, parts - 1),
                0,
                jnp.where(there, step, steps - 1),
            )

    whole = pl.BlockSpec((tokens, D), lambda turn, part, step, place: (0, 0))
    shape = (count, parts, rows, steps * tile)
    return pl.pallas_call(
        partial(pair_kernel, by_rows=by_rows, halves=halves),
        grid_spec=pltpu.PrefetchScalarGridSpec(
            num_scalar_prefetch=1,
            grid=(dp_size, parts, steps),
            in_specs=[
                pl.BlockSpec((D // 2, D), lambda turn, part, step, place: (0, 0)),
                whole,
                whole,
                pl.BlockSpec(right_block, right_place),
                pl.BlockSpec(right_block, right_place),
            ],
            out_specs=[
                pl.BlockSpec((1, 1, rows, tile), near_place),
                pl.BlockSpec((1, 1, rows, tile), away_place),
            ],
            scratch_shapes=[pltpu.VMEM((D // 2, tokens), bfloat)] * 2,
        ),
        out_shape=[
            jax.ShapeDtypeStruct(shape, float32),
            jax.ShapeDtypeStruct(shape, bfloat),
        ],
        cost_estimate=cost(
            flops=2 * tokens * D * dp_size * steps * tile * parts,
            bytes_accessed=4 * D * dp_size * steps * tile * parts,
            transcendentals=0,
        ),
        compiler_params=pltpu.CompilerParams(vmem_limit_bytes=14 * MIB),
    )(wires.dp.reshape(1).astype(jnp.int32), select, left, left_other, right, right_other)


def product_kernel(select_ref, left_ref, left_other_ref, right_ref, right_other_ref, out_ref):
    rows = dot_nt(select_ref[...], left_ref[...]).astype(bfloat)
    rows_other = dot_nt(select_ref[...], left_other_ref[...]).astype(bfloat)
    width = right_ref.shape[-1]
    for part in range(right_ref.shape[0]):
        product = dot_nn(rows, right_ref[part]) + dot_nn(rows_other, right_other_ref[part])
        out_ref[:, part * width : (part + 1) * width] = product.astype(out_ref.dtype)


def pair_product(select, left, right, kind):
    parts, tokens, width = right[0].shape
    return pl.pallas_call(
        product_kernel,
        out_shape=jax.ShapeDtypeStruct((select.shape[0], parts * width), kind),
        cost_estimate=cost(
            flops=2 * tokens * D * parts * width, bytes_accessed=8 * MIB, transcendentals=0
        ),
        compiler_params=pltpu.CompilerParams(vmem_limit_bytes=16 * MIB),
    )(select, *left, *right)


def mixed_kernel(place_ref, away_ref, near_ref, weight_ref, out_ref):
    turn, part = pl.program_id(0), pl.program_id(1)

    @pl.when((turn == 0) & (part == 0))
    def start():
        out_ref[...] = jnp.zeros_like(out_ref)

    @pl.when(turn == 0)
    def away():
        out_ref[...] += dot_nt(away_ref[0], weight_ref[...])

    @pl.when(turn == 1)
    def near():
        out_ref[...] += dot_nt(near_ref[0], weight_ref[...])


def mixed_backward(place, away, near, weight):
    width = away.shape[-1]
    return pl.pallas_call(
        mixed_kernel,
        grid_spec=pltpu.PrefetchScalarGridSpec(
            num_scalar_prefetch=1,
            grid=(2, 3),
            in_specs=[
                pl.BlockSpec(
                    (1, TOKENS, width), lambda turn, part, place: (jnp.where(turn == 0, part, 2), 0, 0)
                ),
                pl.BlockSpec(
                    (1, TOKENS, width), lambda turn, part, place: (jnp.where(turn == 1, part, 0), 0, 0)
                ),
                pl.BlockSpec(
                    (D, width), lambda turn, part, place: (0, 2 * part + (place[0] ^ (1 - turn)))
                ),
            ],
            out_specs=pl.BlockSpec((TOKENS, D), lambda turn, part, place: (0, 0)),
        ),
        out_shape=jax.ShapeDtypeStruct((TOKENS, D), float32),
        cost_estimate=cost(
            flops=6 * TOKENS * D * D, bytes_accessed=10 * MIB, transcendentals=0
        ),
        compiler_params=pltpu.CompilerParams(vmem_limit_bytes=14 * MIB),
    )(place.reshape(1).astype(jnp.int32), away, near, weight)


def fold(values):
    distances, parts, rows, width = values.shape
    return values.transpose(0, 2, 1, 3).reshape(distances, rows, parts * width)


class Flow:
    def __init__(self, wires, plain, exact=None):
        self.wires, self.plain, self.exact, self.sent = wires, plain, exact, []

    @staticmethod
    def halves(values, by_rows):
        if by_rows:
            half = values.shape[1] // 2
            return values[:, :half], values[:, half:]
        values = values.reshape((values.shape[0] // 2, 2) + values.shape[1:])
        return values[:, 0], values[:, 1]

    def send(self, away, away_exact, bit):
        parts = [item.astype(bfloat) for item in away]
        if away_exact is not None:
            parts.append(split_exact(away_exact))
        self.sent.append(jnp.concatenate(parts, axis=-1) if len(parts) > 1 else parts[0])
        return self.wires.swap(self.sent[-1], bit)

    def halved(self, values, bit):
        return (None, None) if values is None else self.halves(values, bit in self.wires.row_bits)

    def finish(self, near, near_exact, got):
        start, sums = 0, []
        for item in near:
            width = item.shape[-1]
            sums.append(item + got[..., start : start + width].astype(float32))
            start += width
        exact = None if near_exact is None else near_exact + joined_exact(got[..., start:])
        return sums, exact

    def land(self, hold=()):
        pairs, near_exact, got = self.pending
        got = after(got, *hold) if hold else got
        self.plain, self.exact = self.finish([near for near, away in pairs], near_exact, got)
        return self

    def next(self, bit, hold=()):
        self.land(hold)
        by_rows = bit in self.wires.row_bits
        pairs = [self.halves(item, by_rows) for item in self.plain]
        near_exact, away_exact = self.halved(self.exact, bit)
        self.pending = (pairs, near_exact, self.send([away for near, away in pairs], away_exact, bit))
        return self

    def first(self, pairs, bit, exact=None):
        near_exact, away_exact = (
            (None, None) if exact is None else self.halves(exact, bit in self.wires.row_bits)
        )
        self.pending = (pairs, near_exact, self.send([away for near, away in pairs], away_exact, bit))
        return self


def gather_relative(wires, values, order):
    for bit in order:
        values = jnp.stack([values, wires.swap(values, bit)])
    return values


def dp_columns(wires, values):
    width = values.shape[-1] // wires.dp_size
    return lax.dynamic_slice_in_dim(values, wires.dp * width, width, values.ndim - 1)


def padded_to(values, width):
    pads = [(0, 0)] * (values.ndim - 1) + [(0, width - values.shape[-1])]
    return jnp.pad(values, pads)


def assemble_kernel(place_ref, *refs, pieces, count):
    outs, ins = refs[count:], refs[:count]
    row, core, dp = place_ref[0], place_ref[1], place_ref[2]
    for source, far_row, far_core, far_dp, start, matrix, offset, width in pieces:
        target = outs[matrix]
        part = target.shape[-1] // 2
        left = pl.multiple_of((dp ^ far_dp) * part + offset, 128)
        for group in range(4):
            target[group, row ^ far_row, core ^ far_core, :, pl.ds(left, width)] = ins[source[0]][
                source[1], group, :, start : start + width
            ]


def doubled(wires, values, bit, hold=()):
    got = wires.swap(values, bit)
    return jnp.stack([values, after(got, *hold) if hold else got])


def in_order(wires, values):
    return jnp.stack(
        [
            lax.dynamic_slice(
                values,
                ((group & 1) ^ wires.bit(wires.near_bit), (group >> 1) ^ wires.bit(wires.far_bit), 0, 0),
                (1, 1) + values.shape[2:],
            )[0, 0]
            for group in range(4)
        ]
    )


class Streams:
    def __init__(self, wires, along, widths, split):
        self.wires, self.widths, self.split = wires, widths, split
        edge = sum(widths[:-1]) + split
        self.first, self.last = along[..., :edge], along[..., edge:]

    def near(self, hold=()):
        wires = self.wires
        self.first = doubled(wires, self.first, wires.row_bits[0], hold)
        self.last = doubled(wires, self.last, wires.dp_bits[0], hold)

    def far(self, hold):
        self.first_far, self.last_far = together(self.first_far, self.last_far, *hold)[:2]

    def swap_near(self):
        self.first_core = self.wires.swap(self.first, self.wires.core_bit)
        self.last_core = self.wires.swap(self.last, self.wires.core_bit)

    def send_far(self):
        wires = self.wires
        self.first_far = wires.swap(self.first, wires.dp_bits[0])
        self.last_far = wires.swap(self.last, wires.row_bits[0])

    def finish(self):
        wires, widths, split = self.wires, self.widths, self.split
        block = self.first.shape[2]
        core_bit = wires.core_bit
        arrays = [
            self.first,
            self.first_far,
            self.last,
            self.last_far,
            self.first_core,
            wires.swap(self.first_far, core_bit),
            self.last_core,
            wires.swap(self.last_far, core_bit),
        ]
        pieces = []
        for far_core in range(2):
            for far in range(2):
                for index in range(2):
                    start = 0
                    for matrix, width in enumerate(widths[:-1] + [split]):
                        source = (4 * far_core + far, index)
                        pieces.append((source, index, far_core, far, start, matrix, 0, width))
                        start += width
                    source = (4 * far_core + 2 + far, index)
                    width = widths[-1] - split
                    pieces.append((source, far, far_core, index, 0, len(widths) - 1, split, width))
        place = jnp.stack(
            [wires.bit(wires.row_bits[0]), wires.bit(wires.core_bit), wires.bit(wires.dp_bits[0])]
        )
        wholes = pl.pallas_call(
            partial(assemble_kernel, pieces=pieces, count=len(arrays)),
            in_specs=[pl.BlockSpec(memory_space=pltpu.SMEM)]
            + [pl.BlockSpec(memory_space=pltpu.VMEM)] * len(arrays),
            out_specs=[pl.BlockSpec(memory_space=pltpu.VMEM)] * len(widths),
            out_shape=[
                jax.ShapeDtypeStruct((4, 2, 2, block, 2 * width), bfloat) for width in widths
            ],
            cost_estimate=cost(
                flops=0, bytes_accessed=4 * D * 2 * sum(widths), transcendentals=0
            ),
            compiler_params=pltpu.CompilerParams(vmem_limit_bytes=16 * MIB),
        )(place.astype(jnp.int32), *arrays)
        return [whole.reshape(D, whole.shape[-1]) for whole in wholes]


def side_by_side(parts, stride, width):
    return padded_to(jnp.concatenate([padded_to(part, stride) for part in parts], axis=-1), width)


def per_device(
    patches,
    masks,
    groups,
    w_square,
    w_qkv,
    w_up,
    w_down,
    small,
    muon_square,
    muon_qkv,
    muon_up,
    muon_down,
    adam_first,
    adam_second,
):
    wires = Wires()
    block = D // wires.fsdp_size
    dp_size = wires.dp_size

    long_image = groups[0] > 0
    patch_limit = jnp.where(long_image, PATCHES, SHORT_PATCHES)
    row = jnp.arange(TOKENS)
    chosen = jnp.pad(masks[0] > 0, (0, TOKENS - PATCHES)) & (row < patch_limit)
    chosen_float = chosen.astype(float32)[:, None]
    mask_local = jnp.sum(chosen_float)

    down_moment, down_master = muon_down.T, w_down.T
    stride = -(-D // dp_size // 128) * 128
    share = max(FF // dp_size, 3 * stride)
    def sub_columns(parts):
        return side_by_side([dp_columns(wires, item) for item in parts], stride, share)

    def thirds(values):
        return [values[:, index * D : (index + 1) * D] for index in range(3)]

    moment_parts = jnp.stack(
        [
            padded_to(dp_columns(wires, down_moment), share),
            sub_columns(thirds(muon_qkv)),
            sub_columns([muon_square[index] for index in range(3)]),
            padded_to(dp_columns(wires, muon_up), share),
        ]
    )
    def for_groups(blocks):
        return [
            lax.dynamic_index_in_dim(blocks, wires.group ^ step, 0, keepdims=False)
            for step in range(4)
        ]

    def send_groups(blocks):
        blocks = for_groups(blocks) if not isinstance(blocks, list) else blocks
        return blocks[:1] + [
            wires.swap_mask(blocks[step], step << wires.near_bit) for step in (1, 2, 3)
        ]

    def by_group(got):
        got = jnp.stack(got)
        return jnp.stack(
            [
                lax.dynamic_index_in_dim(got, group ^ wires.group, 0, keepdims=False)
                for group in range(4)
            ]
        )

    def across_groups(blocks):
        return by_group(send_groups(blocks))

    moment_blocks = for_groups(moment_parts)

    half = SMALL_PAD // 2
    used = -(-SMALL_ROWS // 2)
    small_low = small.astype(bfloat).T
    own_count = jnp.full((block, half - used), mask_local)
    high_count = jnp.floor(own_count / 256.0)
    lane = lax.broadcasted_iota(jnp.int32, own_count.shape, 1)
    spare = jnp.where(lane == 0, high_count, jnp.where(lane == 1, own_count - 256.0 * high_count, 0.0))
    spare = spare.astype(bfloat)
    small_rows = jnp.concatenate(
        [
            small_low[:, :used],
            spare,
            padded_to(small_low[:, used:], used),
            spare,
        ],
        axis=1,
    )
    square_low = w_square.astype(bfloat)
    down_rows = w_down.astype(bfloat).T
    groups_low = [
        [square_low[0], small_rows, w_qkv.astype(bfloat)],
        [square_low[1], w_up.astype(bfloat)],
        [square_low[2], down_rows],
    ]
    half_widths = [[shard.shape[1] // 2 for shard in shards] for shards in groups_low]
    staged = (
        dp_size == 2
        and len(wires.row_bits) == 1
        and not any(width % 128 for widths in half_widths for width in widths)
    )
    if staged:
        near_bit, far_bit = wires.near_bit, wires.far_bit

        def own_columns(shards):
            return jnp.concatenate([dp_columns(wires, shard) for shard in shards], axis=1)

        early_own, middle_own, late_own = [own_columns(shards) for shards in groups_low]
        early_own = doubled(wires, doubled(wires, early_own, far_bit), near_bit)
        early = Streams(wires, in_order(wires, early_own), half_widths[0], 256)
        middle_own = after(middle_own, early.first)
        early.near()
        early.send_far()
        middle_own = doubled(wires, middle_own, far_bit)
        early.swap_near()
        early.far((middle_own, early.first_core, early.last_core, *moment_blocks))
        embed_weight, small_whole, qkv_weight = early.finish()
        counts = small_whole.reshape(D, 2, half)[:, :, used : used + 2].astype(float32)
        mask_count = (256.0 * jnp.sum(counts[:, :, 0]) + jnp.sum(counts[:, :, 1])) / block
    else:
        (embed_weight, small_whole, qkv_weight), (out_weight, up_weight), (
            head_weight,
            down_weight,
        ) = [
            [lax.all_gather(shard, "fsdp", axis=0, tiled=True) for shard in shards]
            for shards in groups_low
        ]
        mask_count = wires.total(jnp.full((8, 128), mask_local))[0, 0]
    params_small = jnp.concatenate(
        [small_whole[:, :used], small_whole[:, half : half + SMALL_ROWS - used]], axis=1
    ).T.astype(float32)

    moments_got = send_groups(moment_blocks)

    long_table, short_table = interp_tables()
    table = jnp.where(long_image, long_table, short_table)
    position = params_small[14 + UP_ROWS : SMALL_ROWS]
    pixels = jnp.pad(patches[0], ((0, TOKENS - PATCHES), (0, 0)))
    is_patch = (row < PATCHES)[:, None]
    is_class = (row == CLASS_ROW)[:, None]
    embedded = jnp.where(
        chosen[:, None], params_small[1], dot_nn(pixels, embed_weight) + params_small[0]
    )
    embedded = jnp.where(is_patch, embedded, jnp.where(is_class, params_small[2], 0.0))
    resid_first = embedded + jnp.dot(table, position, precision=lax.Precision.HIGHEST)
    if staged:
        middle_own = doubled(wires, middle_own, near_bit, (resid_first,))
        middle = Streams(wires, in_order(wires, middle_own), half_widths[1], 512)
        late_own = after(late_own, middle.first, middle.last)
    unit_first, inverse_first = normalized(resid_first)
    normed_first = (unit_first * params_small[3] + params_small[4]).astype(bfloat)
    qkv_bias = jnp.concatenate([params_small[12], jnp.zeros((D,), float32), params_small[13]])
    mixed = (dot_nn(normed_first, qkv_weight) + qkv_bias).astype(bfloat)
    pixels_both = (pixels, wires.swap(pixels, wires.core_bit))
    mixed, *pixels_both = together(mixed, *pixels_both)
    first_both = (normed_first, wires.swap(normed_first, wires.core_bit))
    keep = ((row < patch_limit) | (row == CLASS_ROW)).astype(float32)[:, None]
    if staged:
        late_own = doubled(wires, late_own, far_bit, (mixed,))
        middle.near((mixed,))
        middle.swap_near()
        mixed = after(mixed, middle.first, middle.last, late_own)
        middle.send_far()
    context_low, logsum = attend_forward(mixed, keep)
    context_low, *first_both = together(context_low, *first_both)
    if staged:
        late_own = doubled(wires, late_own, near_bit, (context_low,))
        late = Streams(wires, in_order(wires, late_own), half_widths[2], 512)
        middle.far((context_low, late.first))
        out_weight, up_weight = middle.finish()
    context_both = (context_low, wires.swap(context_low, wires.core_bit))
    resid_second = resid_first + dot_nn(context_low, out_weight) + params_small[5]
    unit_second, inverse_second = normalized(resid_second)
    normed_second = (unit_second * params_small[6] + params_small[7]).astype(bfloat)
    up_bias = params_small[14 : 14 + UP_ROWS].reshape(-1)
    if staged:
        late.near((normed_second,))
        late.swap_near()
        normed_second = after(normed_second, late.first, late.last, late.first_core, late.last_core)
        late.send_far()
    second_both = (normed_second, wires.swap(normed_second, wires.core_bit))
    activ_low, slope = up_forward(normed_second, up_weight, up_bias[None])
    activ_low, moments_got[1], context_other, second_other = together(
        activ_low, moments_got[1], context_both[1], second_both[1]
    )
    context_both, second_both = (context_low, context_other), (normed_second, second_other)
    if staged:
        late.far((activ_low,))
        head_weight, down_weight = late.finish()
    activ_both = (activ_low[None], wires.swap(activ_low, wires.core_bit)[None])
    resid_third = resid_second + dot_nt(activ_low, down_weight) + params_small[8]
    unit_final, inverse_final = normalized(resid_third)
    normed_final = (unit_final * params_small[9] + params_small[10]).astype(bfloat)
    predicted = dot_nn(normed_final, head_weight) + params_small[11]
    residual_error = predicted - pixels.astype(float32)
    loss_local = jnp.sum(chosen_float * residual_error * residual_error)

    core = wires.core_bit
    select = own_selection(wires)

    def other(values):
        return wires.swap(values, core)

    x_order = wires.dp_bits + wires.row_bits
    y_order = wires.row_bits + wires.dp_bits

    def both(values):
        return values, other(values)

    def both(values):
        return values, other(values)

    part_width = D // dp_size

    def blocks(values):
        return values.reshape(4, block, values.shape[-1])

    def wide_part(flows):
        return jnp.concatenate([blocks(item.plain[0]) for item in flows], axis=-1)

    def extra_part(flows):
        return blocks(next(item.plain[1] for item in flows if len(item.plain) > 1))

    near, far = wires.bit(wires.near_bit), wires.bit(wires.far_bit)

    def pick(flag, first, second):
        return jnp.where(flag == 0, first, second)

    class near_stage:
        def __init__(self, first, second, exact=None):
            self.keep, self.exact = pick(near, first, second), None
            parts = [pick(near, second, first).astype(bfloat)]
            if exact is not None:
                self.exact = pick(near, *exact)
                parts.append(split_exact(pick(near, exact[1], exact[0])))
            self.sent = jnp.concatenate(parts, axis=-1)
            self.got = wires.swap(self.sent, wires.near_bit)

        def land(self, hold=()):
            got = after(self.got, *hold) if hold else self.got
            width = self.keep.shape[-1]
            total = self.keep + got[..., :width].astype(float32)
            if self.exact is None:
                return total, None
            return total, self.exact + joined_exact(got[..., width:])

    def flow(pairs, order, exact=None):
        return Flow(wires, None).first(
            [(fold(near), fold(away)) for near, away in pairs], order[0], exact
        )

    def onward(flows, orders, hold=()):
        for item, order in zip(flows, orders):
            for bit in order[1:]:
                item.next(bit, hold)
        return [item.sent[-1] for item in flows]

    grad_pred = 2.0 / mask_count * chosen_float * residual_error
    pred_low = grad_pred.astype(bfloat)
    head_pair = pair_grad(wires, select, both(normed_final), both(pred_low[None]), False)
    grad_head_bias = jnp.sum(grad_pred, axis=0, keepdims=True)
    grad_normed = dot_nt(pred_low, head_weight)
    grad_resid, gain_final, shift_final = norm_backward(
        grad_normed, unit_final, inverse_final, params_small[9]
    )
    branch_low = grad_resid.astype(bfloat)
    branch_both = both(branch_low)
    down_pairs = [
        pair_grad(wires, select, branch_both, activ_both, cut == 1, cut=cut) for cut in range(2)
    ]
    down_flows = [flow([down_pairs[0], head_pair], x_order), flow(down_pairs[1:], y_order)]
    grad_down_bias = jnp.sum(grad_resid, axis=0, keepdims=True)
    hidden_low, grad_up_bias = hidden_backward(
        after(branch_low, *(item.sent[0] for item in down_flows)), down_weight, slope
    )
    hidden_both = both(hidden_low[None])
    grad_normed = dot_nt(hidden_low, up_weight)
    grad_part, gain_second, shift_second = norm_backward(
        grad_normed, unit_second, inverse_second, params_small[6]
    )
    grad_resid = grad_resid + grad_part
    branch_low = grad_resid.astype(bfloat)
    normed_both = second_both
    up_first = pair_grad(
        wires, select, normed_both, (after(hidden_both[0], branch_low), hidden_both[1]), False, cut=0
    )
    up_last = pair_grad(
        wires, select, normed_both, (after(hidden_both[0], up_first[1]), hidden_both[1]), True, cut=1
    )
    out_pair = pair_grad(
        wires, select, context_both, (after(branch_low, up_last[1])[None], other(branch_low)[None]),
        True,
    )
    up_flows = [flow([up_first], x_order), flow([up_last, out_pair], y_order)]
    grad_out_bias = jnp.sum(grad_resid, axis=0, keepdims=True)
    grad_context = dot_nt(after(branch_low, out_pair[1]), out_weight).astype(bfloat)
    sent = onward(down_flows, [x_order, y_order], (grad_context,))
    grad_context = after(grad_context, *sent, *(item.sent[-1] for item in up_flows))
    normed_both = first_both
    if dp_size == 2:
        away_low, away_sums = attend_backward(mixed, grad_context, logsum, keep, 1 - wires.dp, 2)
        away_both = both(away_low)
        for item in down_flows:
            item.land((away_low,))
        sent = onward(up_flows, [x_order, y_order], (away_low, *(item.plain[0] for item in down_flows)))
        away_pair = pair_product(
            select, normed_both, (after(away_both[0], *sent), away_both[1]), bfloat
        )
        grad_context = after(grad_context, away_pair)
        near_low, near_sums = attend_backward(mixed, grad_context, logsum, keep, wires.dp, 2)
        near_both = both(near_low)
        near_pair = pair_product(select, normed_both, near_both, float32)
        qkv_flow = Flow(wires, None).first([(near_pair[None], away_pair[None])], x_order[0])
        grad_normed = mixed_backward(wires.dp, away_low, after(near_low, near_pair), qkv_weight)
        for item in up_flows:
            item.land((grad_normed,))
        wide_near = near_stage(wide_part(down_flows), wide_part(up_flows))
        grad_normed = after(grad_normed, wide_near.sent)
        bias_sums = jnp.where(
            wires.dp == 0,
            jnp.concatenate([near_sums, away_sums], axis=1),
            jnp.concatenate([away_sums, near_sums], axis=1),
        )
    else:
        mixed_low, bias_sums = attend_backward(
            mixed, grad_context, logsum, keep, jnp.zeros((), jnp.int32), 1
        )
        for item in down_flows:
            item.land((mixed_low,))
        sent = onward(up_flows, [x_order, y_order], (mixed_low,))
        qkv_pair = pair_grad(wires, select, normed_both, both(mixed_low), False)
        qkv_flow = flow([qkv_pair], x_order)
        for item in up_flows:
            item.land()
        wide_near = near_stage(wide_part(down_flows), wide_part(up_flows))
        grad_normed = sum(dot_nt(mixed_low[i], thirds(qkv_weight)[i]) for i in range(3))
    grad_part, gain_first, shift_first = norm_backward(
        grad_normed, unit_first, inverse_first, params_small[3]
    )
    grad_resid = grad_resid + grad_part
    unchosen = jnp.where(is_patch & ~chosen[:, None], grad_resid, 0.0)
    unchosen_low = unchosen.astype(bfloat)
    unchosen_both = both(unchosen_low[None])
    sent = onward([qkv_flow], [x_order], (unchosen_low,))
    grad_resid = after(grad_resid, *sent)
    grad_leading = grad_resid[CLASS_ROW : CLASS_ROW + 1]
    grad_position = lax.dot_general(
        table, grad_resid, (((0,), (0,)), ((), ())), precision=lax.Precision.HIGHEST
    )
    grad_mask_token = jnp.sum(jnp.where(chosen[:, None], grad_resid, 0.0), axis=0, keepdims=True)
    grad_patch_bias = jnp.sum(unchosen, axis=0, keepdims=True)
    small_parts = [
        grad_patch_bias,
        grad_mask_token,
        grad_leading,
        gain_first,
        shift_first,
        grad_out_bias,
        gain_second,
        shift_second,
        grad_down_bias,
        gain_final,
        shift_final,
        grad_head_bias,
        bias_sums,
        grad_up_bias.reshape(UP_ROWS, D),
        grad_position,
    ]
    small_parts[-1] = after(grad_position, unchosen_both[1])
    grad_small = stacked_rows(small_parts, SMALL_PAD)

    wide_half, unused = wide_near.land((grad_small,))
    wide_far = wide_half.astype(bfloat)
    far_mask = 1 << wires.far_bit
    places = [((i >> wires.near_bit) & 1, (i >> wires.far_bit) & 1, i) for i in range(wires.count)]
    wide_got = lax.ppermute(
        wide_far, BOTH, [(i, i ^ far_mask) for n, f, i in places if n != f]
    )
    unchosen_both = (after(unchosen_both[0], wide_far), unchosen_both[1])
    patch_pair = pair_grad(wires, select, pixels_both, unchosen_both, False)

    tail = half // dp_size
    grad_small = grad_small + other(grad_small)
    grad_small = grad_small.reshape(2, dp_size, tail, D)
    grad_small = jnp.stack(
        [
            lax.dynamic_index_in_dim(grad_small, wires.dp ^ distance, 1, keepdims=False)
            for distance in range(dp_size)
        ]
    ).reshape(SMALL_PAD, D)
    layers, rest = [], grad_small
    for layer in range(3):
        layers.append(rest.astype(bfloat))
        rest = rest - layers[-1].astype(float32)
    small_own = sum(dot_nt(select, layer) for layer in layers)
    small_own = small_own.reshape(D // 2, dp_size, 2 * tail).transpose(1, 0, 2)
    patch_flow = flow([patch_pair], x_order, small_own)
    qkv_flow.land((patch_flow.sent[0],))
    onward([patch_flow], [x_order], (moments_got[2], *qkv_flow.plain))
    patch_flow.land((moments_got[3],))

    qkv_part = blocks(qkv_flow.plain[0])
    square_part = jnp.concatenate(
        [blocks(patch_flow.plain[0]), extra_part(up_flows), extra_part(down_flows)], axis=-1
    )
    small_part = blocks(patch_flow.exact)
    small_low_part, small_high_part = small_part[..., :tail], small_part[..., tail:]
    wide_sum = wide_half + after(wide_got, *patch_flow.sent).astype(float32)
    narrow_sum, small_sum = near_stage(
        after(square_part, wide_sum), qkv_part, (small_low_part, small_high_part)
    ).land()
    narrow_got = lax.ppermute(
        jnp.concatenate([narrow_sum.astype(bfloat), split_exact(small_sum)], axis=-1),
        BOTH,
        [(i, i ^ far_mask) for n, f, i in places if n == f],
    )
    narrow_sum = narrow_sum + narrow_got[..., : 3 * part_width].astype(float32)
    small_sum = small_sum + joined_exact(narrow_got[..., 3 * part_width :])
    narrow_sum = side_by_side(
        [narrow_sum[..., i * part_width : (i + 1) * part_width] for i in range(3)], stride, share
    )
    outer = near ^ far
    own_grad = pick(outer, padded_to(wide_sum, share), narrow_sum)
    own_small = pick(outer, jnp.zeros_like(small_sum), small_sum)
    own_grad, own_small = lax.optimization_barrier((own_grad, own_small))


    squares_local = jnp.sum(own_grad * own_grad) + jnp.sum(own_small * own_small)
    lane = lax.broadcasted_iota(jnp.int32, (8, 128), 1)
    scalars = wires.total(jnp.where(lane == 0, loss_local, squares_local))
    loss_sum = scalars[0, 0]
    grad_norm = jnp.sqrt(scalars[0, 1])
    factor = jnp.minimum(1.0, clip_limit / (grad_norm + 1e-06))

    own_moment = by_group(moments_got)
    grad_blocks = jnp.concatenate([own_grad.astype(bfloat), split_exact(own_small)], axis=-1)
    grad_blocks = after(grad_blocks, factor)
    grads_got = send_groups(grad_blocks)
    clipped = own_grad * factor
    blend = clipped + momentum_decay * (momentum_decay * own_moment + clipped)
    blend_low = blend.astype(bfloat)
    half_rows = 2 * block
    dps, rows = wires.dp_bits, wires.row_bits
    upper, lower = blend_low[:2].reshape(half_rows, share), blend_low[2:].reshape(half_rows, share)
    orders = list(zip(dps + rows, rows + dps))
    for turn, (upper_bit, lower_bit) in enumerate(orders):
        upper_got, lower_got = wires.swap(upper, upper_bit), wires.swap(lower, lower_bit)
        if turn < 2:
            upper_got, lower_got, grads_got[turn + 1] = together(
                upper_got, lower_got, grads_got[turn + 1]
            )
        upper, lower = jnp.stack([upper, upper_got]), jnp.stack([lower, lower_got])
    own_pieces = jnp.concatenate(
        [upper.reshape(-1, half_rows, share), lower.reshape(-1, half_rows, share)]
    )
    other_pieces = other(own_pieces)
    squares_flag = (wires.group == 2).astype(jnp.int32).reshape(1)
    ortho = orthogonalize(
        squares_flag, own_pieces, other_pieces, 1 << len(rows), dp_size, stride, 4 * block
    )

    ortho, grads_got[3] = together(ortho, grads_got[3])
    grad_rows = by_group(grads_got)
    grad_all = gather_relative(wires, grad_rows, dps).reshape((dp_size,) + grad_rows.shape)

    updates_got = send_groups(ortho.reshape(4, block, ortho.shape[1]))

    def joined(parts):
        parts = jnp.stack(parts)
        return jnp.concatenate(
            [
                lax.dynamic_index_in_dim(parts, place ^ wires.dp, 0, keepdims=False)
                for place in range(dp_size)
            ],
            axis=-1,
        ).astype(float32)

    def grad_columns(task, start, width):
        part = width // dp_size
        return joined([grad_all[far, task, :, start : start + part] for far in range(dp_size)])

    def update_columns(task, start, width, spread):
        part = width // dp_size
        return joined(
            [
                updates[task, :, far * spread + start : far * spread + start + part]
                for far in range(dp_size)
            ]
        )

    def three_grads(task):
        return [grad_columns(task, index * stride, D) for index in range(3)]

    grads = [
        jnp.stack(three_grads(2)),
        jnp.concatenate(three_grads(1), axis=1),
        grad_columns(3, 0, FF),
        grad_columns(0, 0, FF),
    ]
    olds = [muon_square, muon_qkv, muon_up, down_moment]
    masters = [w_square, w_qkv, w_up, down_master]
    new_moments = [
        momentum_decay * old + factor * fresh for old, fresh in zip(olds, grads)
    ]
    small_grad = jnp.concatenate(
        [
            grad_columns(task, share, half) + grad_columns(task, share + tail, half)
            for task in (2, 1)
        ],
        axis=1,
    )[:, :SMALL_ROWS].T
    small_grad = small_grad * factor
    new_first = beta_first * adam_first + (1.0 - beta_first) * small_grad
    new_second = beta_second * adam_second + (1.0 - beta_second) * small_grad * small_grad
    first_hat = new_first / (1.0 - beta_first**STEP)
    second_hat = new_second / (1.0 - beta_second**STEP)
    new_small = small - adam_rate * first_hat / (jnp.sqrt(second_hat) + adam_eps)
    early_outs = (*new_moments, new_small, new_first, new_second)
    updates_got, early_outs = lax.optimization_barrier((updates_got, early_outs))
    *new_moments, new_small, new_first, new_second = early_outs
    updates = by_group(updates_got)
    ups = [
        jnp.stack([update_columns(2, index * dp_size * stride, D, stride) for index in range(3)]),
        jnp.concatenate(
            [update_columns(1, index * stride, D, share) for index in range(3)], axis=1
        ),
        update_columns(3, 0, FF, share),
        update_columns(0, 0, FF, share),
    ]
    new_weights = [
        master * (1.0 - muon_rate * muon_decay)
        - muon_rate * 0.2 * math.sqrt(master.shape[-1]) * update
        for master, update in zip(masters, ups)
    ]
    return (
        loss_sum,
        mask_count,
        grad_norm,
        new_weights[0],
        new_moments[0],
        new_weights[1],
        new_moments[1],
        new_weights[2],
        new_moments[2],
        new_weights[3].T,
        new_moments[3].T,
        new_small,
        new_first,
        new_second,
    )


def solution(mesh):
    placed = (
        P(("fsdp", "dp"), None, None),
        P(("fsdp", "dp"), None),
        P(("fsdp", "dp")),
        P(None, "fsdp", None),
        P("fsdp", None),
        P("fsdp", None),
        P(None, "fsdp"),
        P(None, "fsdp"),
        P(None, "fsdp", None),
        P("fsdp", None),
        P("fsdp", None),
        P(None, "fsdp"),
        P(None, "fsdp"),
        P(None, "fsdp"),
    )
    return jax.shard_map(
        per_device,
        mesh=mesh,
        in_specs=placed,
        out_specs=(
            P(),
            P(),
            P(),
            P(None, "fsdp", None),
            P(None, "fsdp", None),
            P("fsdp", None),
            P("fsdp", None),
            P("fsdp", None),
            P("fsdp", None),
            P(None, "fsdp"),
            P(None, "fsdp"),
            P(None, "fsdp"),
            P(None, "fsdp"),
            P(None, "fsdp"),
        ),
        check_vma=False,
    )
```
